512 devices in a mesh: scen: 4 (over x), gx: 8 (over y, core), gy: 16 (over z).
Axes of the slice: x: 4, y: 4, z: 16, core: 2. Of those that a mesh axis runs over, the one named last changes fastest.
Arguments:
- perm_log: float32 [2, 512, 2048], P(None, 'gx', 'gy'), may hold values from -2.5 to 2.5
- facies: int32 [2, 512, 2048], P(None, 'gx', 'gy'), may hold values from 0 to 3
- facies_scale: float32 [4], replicated, may hold values from 0.5 to 2
- accumulation: float32 [2, 512, 2048], P(None, 'gx', 'gy'), may hold values from 0.05 to 0.5
- previous_pressure: float32 [4, 2, 512, 2048], P('scen', None, 'gx', 'gy'), may hold values from -6 to 6
- observed: float32 [4, 2, 512, 2048], P('scen', None, 'gx', 'gy'), may hold values from -6 to 6
- well_cells: int32 [4, 5], P('scen'), may hold values from 0 to 2097151
- well_rates: float32 [4, 5], P('scen'), may hold values from 5 to 20
Outputs:
- pressure: float32 [4, 2, 512, 2048], P('scen', None, 'gx', 'gy')
- adjoint: float32 [4, 2, 512, 2048], P('scen', None, 'gx', 'gy')
- gradient: float32 [2, 512, 2048], P(None, 'gx', 'gy')
The draws below stay inside these ranges and needn't reach their ends.
Inputs may be any that keep to these rules, and one draw needn't show every extreme that they name: `well_cells`: a flat index layer * 512 * 2048 + row * 2048 + column of a grid cell; several wells may share a cell.
All inputs are finite; a program needn't handle non-finite values.
Results may differ from the reference program's by a relative error of at most 0.0001.
Values sent between devices are 32-bit elements; how exact they have to be, the bound alone decides.
A program may use at most 128 MiB of HBM per device.

```python
import math
import jax
import jax.numpy as jnp

LZ = 2
WELLS = 5
FACIES = 4
SMOOTH = 2
COARSE = 4
SCEN = 4
NX = 512
NY = 2048


def touch_ends(values, own_key, least, high):
    index_at = [jax.random.randint(jax.random.fold_in(own_key, axis), (), 0, length) for axis, length in enumerate(values.shape)]
    main_axis = values.shape.index(max(values.shape))
    beside = index_at[:main_axis] + [(index_at[main_axis] + 1) % values.shape[main_axis]] + index_at[main_axis + 1:]
    return values.at[tuple(index_at)].set(least).at[tuple(beside)].set(high)


def levels(stream_key, shape, shards, smallest, high):
    def one(axis_at, parts):
        heights = jax.random.uniform(jax.random.fold_in(jax.random.fold_in(stream_key, 6), axis_at), (parts,), jnp.float32, smallest / len(shards), high / len(shards))
        return jnp.repeat(jnp.exp(heights), shape[axis_at] // parts).reshape((-1,) + (1,) * (len(shape) - axis_at - 1))

    factor_of = one(*shards[0])
    for cut in shards[1:]:
        factor_of = factor_of * one(*cut)
    return factor_of


def scatter_about(rng, extent, width, most, cuts=(), kind=jnp.bfloat16):
    drawn = jax.random.normal(rng, extent, jnp.float32) * width
    if len(cuts) > 0:
        drawn = levels(rng, extent, cuts, -0.22, 0.18) * drawn
    return jnp.clip(drawn, min=-most, max=most).astype(kind)


def setup_inputs(seed: int = 0) -> dict:
    arg_keys = jax.random.split(jax.random.key(seed), 9)
    return {
        "perm_log": scatter_about(arg_keys[0], (LZ, NX, NY), 0.7, 2.5, ((1, 8), (2, 16)), jnp.float32),
        "facies": touch_ends(jax.random.randint(arg_keys[1], (LZ, NX, NY), 0, FACIES), jax.random.fold_in(arg_keys[1], 1), 0, FACIES - 1).astype(jnp.int32),
        "facies_scale": jnp.clip(jnp.exp(jax.random.uniform(arg_keys[2], (FACIES,), jnp.float32, math.log(0.5), math.log(2.0))), 0.5, 2.0),
        "accumulation": jnp.clip(jnp.exp(math.log(0.5) - 2.3025851 * jax.random.uniform(arg_keys[3], (LZ, NX, NY), jnp.float32) ** levels(arg_keys[3], (LZ, NX, NY), ((1, 8), (2, 16)), -0.2, 0.2)), 0.05, 0.5),
        "previous_pressure": scatter_about(arg_keys[4], (SCEN, LZ, NX, NY), 1.0, 6.0, ((0, 4), (2, 8), (3, 16)), jnp.float32),
        "observed": scatter_about(arg_keys[5], (SCEN, LZ, NX, NY), 1.0, 6.0, ((0, 4), (2, 8), (3, 16)), jnp.float32),
        "well_cells": touch_ends(jax.random.randint(arg_keys[6], (SCEN, WELLS), 0, LZ * NX * NY), jax.random.fold_in(arg_keys[6], 1), 0, (LZ * NX * NY) - 1).astype(jnp.int32),
        "well_rates": jnp.clip(5.0 + 15.0 * jax.random.uniform(arg_keys[7], (SCEN, WELLS), jnp.float32) ** levels(arg_keys[7], (SCEN, WELLS), ((0, 4),), -0.2, 0.2), 5.0, 20.0),
    }


vertical = 0.3
damping = 0.8


def harmonic(left, right):
    return 2.0 * left * right / (left + right)


def planar(padded):
    return (padded[..., :-2, 1:-1], padded[..., 2:, 1:-1], padded[..., 1:-1, :-2], padded[..., 1:-1, 2:])


def layer_pair(values):
    padded = jnp.pad(values, ((1, 1), (0, 0), (0, 0)))
    return padded[:-2], padded[2:]


def padded_neighbours(values):
    return planar(jnp.pad(values, ((0, 0), (1, 1), (1, 1))))


def build_coeffs(permeability, beside, accumulation):
    below, above = layer_pair(permeability)
    return jnp.stack([harmonic(permeability, beside[0]), harmonic(permeability, beside[1]),
                      harmonic(permeability, beside[2]), harmonic(permeability, beside[3]),
                      vertical * harmonic(permeability, below), vertical * harmonic(permeability, above),
                      accumulation])


def coarsen(coeffs):
    member_count, layer_count, row_count, col_count = coeffs.shape
    quads = coeffs.reshape(member_count, layer_count, row_count // 2, 2, col_count // 2, 2)
    return jnp.stack([quads[0, :, :, 0, :, 0] + quads[0, :, :, 0, :, 1],
                      quads[1, :, :, 1, :, 0] + quads[1, :, :, 1, :, 1],
                      quads[2, :, :, 0, :, 0] + quads[2, :, :, 1, :, 0],
                      quads[3, :, :, 0, :, 1] + quads[3, :, :, 1, :, 1],
                      jnp.sum(quads[4], (2, 4)), jnp.sum(quads[5], (2, 4)), jnp.sum(quads[6], (2, 4))])


def restrict(values):
    layer_count, row_count, col_count = values.shape
    return values.reshape(layer_count, row_count // 2, 2, col_count // 2, 2).sum((2, 4))


def upsample(values):
    return jnp.repeat(jnp.repeat(values, 2, 1), 2, 2)


def apply_op(values, grid_level):
    coeffs, diagonal = grid_level
    row_lo, row_hi, col_lo, col_hi = padded_neighbours(values)
    layer_lo, layer_hi = layer_pair(values)
    return diagonal * values - (coeffs[0] * row_lo + coeffs[1] * row_hi + coeffs[2] * col_lo
                                + coeffs[3] * col_hi + coeffs[4] * layer_lo + coeffs[5] * layer_hi)


def smooth(values, target, grid_level, sweeps):
    for _ in range(sweeps):
        values = values + damping * (target - apply_op(values, grid_level)) / grid_level[1]
    return values


def vcycle(target, initial, grids):
    finest, middle, bottom = grids
    fine_field = smooth(initial, target, finest, SMOOTH)
    middle_target = restrict(target - apply_op(fine_field, finest))
    middle_field = smooth(jnp.zeros_like(middle_target), middle_target, middle, SMOOTH)
    bottom_target = restrict(middle_target - apply_op(middle_field, middle))
    bottom_field = smooth(jnp.zeros_like(bottom_target), bottom_target, bottom, COARSE)
    middle_field = smooth(middle_field + upsample(bottom_field), middle_target, middle, SMOOTH)
    fine_field = fine_field + upsample(middle_field)
    return smooth(fine_field, target, finest, SMOOTH)


def face_term(permeability, perm_side, pressure, pressure_side, adjoint, adjoint_side, weight):
    total_perm = permeability + perm_side
    return weight * permeability * 2.0 * perm_side * perm_side / (total_perm * total_perm) * (adjoint - adjoint_side) * (pressure - pressure_side)


def gradient_terms(permeability, perm_six, pressure, pressure_six, adjoint, adjoint_six):
    weights = (1.0, 1.0, 1.0, 1.0, vertical, vertical)
    total = jnp.zeros_like(permeability)
    for number in range(6):
        total = total + face_term(permeability, perm_six[number], pressure, pressure_six[number],
                                  adjoint, adjoint_six[number], weights[number])
    return total


def with_diagonal(coeffs):
    return (coeffs, jnp.sum(coeffs, 0))


def reference(perm_log, facies, facies_scale, accumulation, previous_pressure, observed, well_cells, well_rates):
    facies_factor = jnp.zeros_like(perm_log)
    for label in range(FACIES):
        facies_factor = facies_factor + jnp.where(facies == label, facies_scale[label], jnp.float32(0.0))
    permeability = jnp.exp(perm_log) * facies_factor
    coeffs = build_coeffs(permeability, padded_neighbours(permeability), accumulation)
    middle = coarsen(coeffs)
    bottom = coarsen(middle)
    grids = (with_diagonal(coeffs), with_diagonal(middle), with_diagonal(bottom))
    perm_six = padded_neighbours(permeability) + layer_pair(permeability)
    total = jnp.zeros_like(permeability)
    pressures = []
    adjoints = []
    for scenario in range(SCEN):
        source = jnp.zeros((LZ * NX * NY,), perm_log.dtype).at[well_cells[scenario]].add(well_rates[scenario]).reshape(LZ, NX, NY)
        pressure = vcycle(accumulation * previous_pressure[scenario] + source, previous_pressure[scenario], grids)
        adjoint = vcycle(pressure - observed[scenario], jnp.zeros_like(pressure), grids)
        total = total + gradient_terms(permeability, perm_six, pressure,
                                       padded_neighbours(pressure) + layer_pair(pressure),
                                       adjoint, padded_neighbours(adjoint) + layer_pair(adjoint))
        pressures.append(pressure)
        adjoints.append(adjoint)
    return jnp.stack(pressures), jnp.stack(adjoints), -total
```

```python
from functools import partial

import jax
import jax.numpy as jnp
from jax import lax
from jax.experimental import pallas as pl
from jax.experimental.pallas import tpu as pltpu
from jax.sharding import PartitionSpec as P

WELLS = 5
FACIES = 4
VERTICAL = 0.3
DAMPING = 0.8
ROWS = 64
LANES = 128
HALO = 32
GUARD = 8
MESH = pl.DeviceIdType.MESH

TOP = (GUARD + HALO, GUARD + HALO // 2, GUARD + HALO // 4)
HEIGHT = tuple(ROWS // 2**k + 2 * TOP[k] for k in range(3))
CHUNK = 16


def over(level, low, high, body, step=CHUNK):
    base = TOP[level]
    for row in range(low, high, step):
        body(base + row, min(step, high - row))


def lanes_of(count):
    return lax.broadcasted_iota(jnp.int32, (count, LANES), 1)


def turn(value, shift):
    return pltpu.roll(value, shift % LANES, 1)


def to_right(m0, m1, h, hs, m1s, lane, s):
    return (
        turn(jnp.where(lane < s, h, m0), -s),
        turn(jnp.where(lane < s, hs, m1), -s),
        turn(jnp.where(lane < s, m0, jnp.where((lane >= 64) & (lane < 64 + s), m1s, h)), -s),
    )


def to_left(m0, m1, h, hs, m1s, lane, s):
    return (
        turn(jnp.where(lane >= LANES - s, h, m0), s),
        turn(jnp.where(lane >= LANES - s, hs, m1), s),
        turn(jnp.where(lane >= LANES - s, m0, jnp.where((lane >= 64 - s) & (lane < 64), m1s, h)), s),
    )


def tiles(ref, row, count):
    return tuple(ref[t, pl.ds(row, count), :] for t in range(3))


def change(v, g, e, level, row, count):
    s = 2**level
    lane = lanes_of(count)
    m0, m1, h = tiles(v, row, count)
    hs, m1s = turn(h, 64), turn(m1, 64)
    right = to_right(m0, m1, h, hs, m1s, lane, s)
    left = to_left(m0, m1, h, hs, m1s, lane, s)
    across = (m1, m0, hs)
    up = tiles(v, row - 1, count)
    down = tiles(v, row + 1, count)
    mid = (m0, m1, h)
    rows = pl.ds(row, count)
    out = []
    for t in range(3):
        near = e[0, t, rows, :] * up[t] + e[1, t, rows, :] * down[t]
        side = e[2, t, rows, :] * right[t] + e[3, t, rows, :] * left[t]
        out.append(
            (near + side) + (e[4, t, rows, :] * across[t] + (g[t, rows, :] - DAMPING * mid[t]))
        )
    return out, mid


def sweep(v, out, g, e, level, low, high):
    def body(row, count):
        delta, mid = change(v, g, e, level, row, count)
        for t in range(3):
            out[t, pl.ds(row, count), :] = mid[t] + delta[t]

    over(level, low, high, body)


def residual(v, out, g, e, level, low, high):
    def body(row, count):
        delta, _ = change(v, g, e, level, row, count)
        for t in range(3):
            out[t, pl.ds(row, count), :] = delta[t] * e[6, t, pl.ds(row, count), :]

    over(level, low, high, body)


def pair_sum(value, lane, s):
    both = value + turn(value, -s)
    return jnp.where(lane % (2 * s) < s, both, turn(both, s))


def even_odd(ref, index, row, count):
    first = ref[(*index, pl.ds(row, count, stride=2), slice(None))]
    second = ref[(*index, pl.ds(row + 1, count, stride=2), slice(None))]
    return first, second


def restrict(fine, g, e, level, low, high):
    s = 2 ** (level - 1)

    def body(row, count):
        lane = lanes_of(count)
        source = TOP[level - 1] + 2 * (row - TOP[level])
        for t in range(3):
            first, second = even_odd(fine, (t,), source, count)
            g[t, pl.ds(row, count), :] = pair_sum(first + second, lane, s) * e[5, t, pl.ds(row, count), :]

    over(level, low, high, body)


def prolong(coarse, fine, level, low, high):
    def body(row, count):
        target = TOP[level - 1] + 2 * (row - TOP[level])
        for t in range(3):
            value = coarse[t, pl.ds(row, count), :]
            for k in range(2):
                rows = pl.ds(target + k, count, stride=2)
                fine[t, rows, :] = fine[t, rows, :] + value

    over(level, low, high, body)


def coarsen(fine, coarse, level, low, high):
    s = 2 ** (level - 1)

    def body(row, count):
        lane = lanes_of(count)
        source = TOP[level - 1] + 2 * (row - TOP[level])
        rows = pl.ds(row, count)
        for t in range(3):
            first, second = even_odd(fine, (0, t), source, count)
            total = first + second
            coarse[0, t, rows, :] = jnp.where(lane % (2 * s) < s, turn(total, -s), total)
            second = fine[1, t, pl.ds(source + 1, count, stride=2), :]
            coarse[1, t, rows, :] = pair_sum(second, lane, s)
            for k in (2, 3):
                first, second = even_odd(fine, (k, t), source, count)
                coarse[k, t, rows, :] = pair_sum(first + second, lane, s)

    over(level, low, high, body)


def scale(faces, e, level, low, high):
    s = 2**level

    def body(row, count):
        lane = lanes_of(count)
        rows = pl.ds(row, count)
        east = tiles(faces.at[0], row, count)
        west = to_left(*east, turn(east[2], 64), turn(east[1], 64), lane, s)
        for t in range(3):
            south = faces[1, t, rows, :]
            north = faces[1, t, pl.ds(row - 1, count), :]
            across = faces[2, t, rows, :]
            diag = ((north + south) + (east[t] + west[t])) + (across + faces[3, t, rows, :])
            w = DAMPING / diag
            e[0, t, rows, :] = w * north
            e[1, t, rows, :] = w * south
            e[2, t, rows, :] = w * east[t]
            e[3, t, rows, :] = w * west[t]
            e[4, t, rows, :] = w * across
            e[5, t, rows, :] = w
            e[6, t, rows, :] = diag * (1.0 / DAMPING)

    over(level, low, high, body)


def harmonic(left, right):
    return 2.0 * left * right / (left + right)


def fine_faces(perm, faces, gx, gy, nx, ny, low, high):
    def body(row, count):
        lane = lanes_of(count)
        at = lax.broadcasted_iota(jnp.int32, (count, LANES), 0) + (row - TOP[0])
        m0, m1, h = tiles(perm, row, count)
        hs, m1s = turn(h, 64), turn(m1, 64)
        right = to_right(m0, m1, h, hs, m1s, lane, 1)
        below = tiles(perm, row + 1, count)
        wall = ((at == -1) & (gx == 0)) | ((at == ROWS - 1) & (gx == nx - 1))
        east = (lane == LANES - 1) & (gy == ny - 1)
        west = ((lane == LANES - 1) | (lane == 63)) & (gy == 0)
        own = (m0, m1, h)
        for t in range(3):
            edge = west if t == 2 else east
            faces[0, t, pl.ds(row, count), :] = jnp.where(edge, 0.0, harmonic(own[t], right[t]))
            faces[1, t, pl.ds(row, count), :] = jnp.where(wall, 0.0, harmonic(own[t], below[t]))
        between = VERTICAL * harmonic(m0, m1)
        faces[2, 0, pl.ds(row, count), :] = between
        faces[2, 1, pl.ds(row, count), :] = between
        faces[2, 2, pl.ds(row, count), :] = VERTICAL * harmonic(h, hs)

    over(0, low, high, body)


def vcycle(levels, spare, last):
    (e0, g0), (e1, g1), (e2, g2) = levels
    va, vb, r0, ua, ub, r1, wa, wb = spare
    sweep(va, vb, g0, e0, 0, -32, 96)
    residual(vb, r0, g0, e0, 0, -24, 88)
    restrict(r0, g1, e1, 1, -16, 48)
    sweep(g1, ub, g1, e1, 1, -16, 48)
    residual(ub, r1, g1, e1, 1, -16, 48)
    restrict(r1, g2, e2, 2, -8, 24)
    sweep(g2, wa, g2, e2, 2, -8, 24)
    sweep(wa, wb, g2, e2, 2, -8, 24)
    sweep(wb, wa, g2, e2, 2, -8, 24)
    prolong(wa, ub, 2, -4, 20)
    sweep(ub, ua, g1, e1, 1, -8, 40)
    sweep(ua, ub, g1, e1, 1, -8, 40)
    prolong(ub, vb, 1, -8, 40)
    sweep(vb, va, g0, e0, 0, -8, 72)
    sweep(va, last, g0, e0, 0, -8, 72)


def pack(m0, m1, to_west, to_east, index):
    lane = lanes_of(32)
    m1s = turn(m1, 64)
    outer = lane % 64 < 32
    for source, target, keep in (
        (jnp.where(lane < 64, m0, m1s), to_west, outer),
        (jnp.where(lane < 64, m1s, m0), to_east, jnp.logical_not(outer)),
    ):
        target[index] = jnp.where(keep[:16], source[:16], turn(source[16:], 32))


def unpack(from_west, from_east, target, source_index, row):
    outer = lanes_of(16) % 64 < 32
    west, east = from_west[source_index], from_east[source_index]
    target[pl.ds(row, 16), :] = jnp.where(outer, east, west)
    target[pl.ds(row + 16, 16), :] = turn(jnp.where(outer, west, east), -32)


def kernel(
    perm_log, facies, facies_scale, accumulation, previous, observed, well_cells, well_rates,
    pressure_out, adjoint_out, gradient_out,
    log_v, facies_v, observed_v, ext, ext2, to_west, to_east, from_west, from_east,
    to_west2, to_east2, from_west2, from_east2,
    f0, f1, f2, e0, e1, e2, g0, g1, g2, va, vb, r0, ua, ub, r1, wa, wb, pv, terms, total,
    load_sem, store_sem, send1, recv1, send2, recv2, send3, recv3,
):
    nx, ny, ns = lax.axis_size("gx"), lax.axis_size("gy"), lax.axis_size("scen")
    gx, gy, me = lax.axis_index("gx"), lax.axis_index("gy"), lax.axis_index("scen")
    north, south = lax.rem(gx + nx - 1, nx), lax.rem(gx + 1, nx)
    west, east = lax.rem(gy + ny - 1, ny), lax.rem(gy + 1, ny)
    around = [
        {"gx": north}, {"gx": south}, {"gy": west}, {"gy": east},
        {"gx": north, "gy": west}, {"gx": north, "gy": east},
        {"gx": south, "gy": west}, {"gx": south, "gy": east},
    ]
    peers = [{"scen": lax.rem(me + k, ns)} for k in range(1, ns)]

    own = pl.ds(TOP[0], ROWS)
    loads = [
        pltpu.make_async_copy(perm_log, log_v, load_sem.at[0]),
        pltpu.make_async_copy(facies, facies_v, load_sem.at[1]),
        pltpu.make_async_copy(accumulation, ext.at[1, 0:2, own, :], load_sem.at[2]),
        pltpu.make_async_copy(previous.at[0], ext.at[2, 0:2, own, :], load_sem.at[3]),
        pltpu.make_async_copy(observed.at[0], observed_v, load_sem.at[4]),
    ]
    for copy in loads:
        copy.start()
    barrier = pltpu.get_barrier_semaphore()
    for target in around + peers:
        pl.semaphore_signal(barrier, inc=1, device_id=target, device_id_type=MESH)

    for copy in loads[:4]:
        copy.wait()
    for layer in range(2):
        labels = facies_v[layer]
        factor = jnp.zeros((ROWS, LANES), jnp.float32)
        for label in range(FACIES):
            factor = jnp.where(labels == label, facies_scale[label], factor)
        ext[0, layer, own, :] = jnp.exp(log_v[layer]) * factor
    for field in range(3):
        for half in range(2):
            rows = pl.ds(TOP[0] + 32 * half, 32)
            pack(ext[field, 0, rows, :], ext[field, 1, rows, :], to_west, to_east, (field, pl.ds(16 * half, 16), slice(None)))
    pl.semaphore_wait(barrier, len(around) + len(peers))

    def exchange(block, w_out, e_out, w_in, e_in, send, recv):
        upper, lower = pl.ds(TOP[0], HALO), pl.ds(TOP[0] + ROWS - HALO, HALO)
        above, below = pl.ds(GUARD, HALO), pl.ds(TOP[0] + ROWS, HALO)
        first, second = pl.ds(0, 16), pl.ds(16, 16)
        lead = (slice(None),) * (len(w_out.shape) - 2)
        pairs = [
            (block.at[(*lead, slice(0, 2), upper)], block.at[(*lead, slice(0, 2), below)]),
            (block.at[(*lead, slice(0, 2), lower)], block.at[(*lead, slice(0, 2), above)]),
            (w_out, e_in.at[(*lead, pl.ds(16, 32))]),
            (e_out, w_in.at[(*lead, pl.ds(16, 32))]),
            (w_out.at[(*lead, first)], e_in.at[(*lead, pl.ds(48, 16))]),
            (e_out.at[(*lead, first)], w_in.at[(*lead, pl.ds(48, 16))]),
            (w_out.at[(*lead, second)], e_in.at[(*lead, pl.ds(0, 16))]),
            (e_out.at[(*lead, second)], w_in.at[(*lead, pl.ds(0, 16))]),
        ]
        copies = [
            pltpu.make_async_remote_copy(
                src_ref=source, dst_ref=target, send_sem=send.at[k], recv_sem=recv.at[k],
                device_id=around[k], device_id_type=MESH,
            )
            for k, (source, target) in enumerate(pairs)
        ]
        for k in (4, 5, 6, 7, 2, 3, 0, 1):
            copies[k].start()
        return copies

    copies1 = exchange(ext, to_west, to_east, from_west, from_east, send1, recv1)
    for copy in copies1:
        copy.wait_recv()
    for field in range(3):
        for block in range(4):
            unpack(from_west, from_east, ext.at[field, 2], (field, pl.ds(16 * block, 16), slice(None)), GUARD + 32 * block)

    perm, accu, start = ext.at[0], ext.at[1], ext.at[2]
    fine_faces(perm, f0, gx, gy, nx, ny, -32, 96)

    def keep_accumulation(row, count):
        for t in range(3):
            f0[3, t, pl.ds(row, count), :] = accu[t, pl.ds(row, count), :]

    over(0, -32, 96, keep_accumulation)
    coarsen(f0, f1, 1, -16, 48)
    coarsen(f1, f2, 2, -8, 24)
    scale(f0, e0, 0, -32, 96)
    scale(f1, e1, 1, -16, 48)
    scale(f2, e2, 2, -8, 24)

    plane, width = nx * ROWS * ny * LANES, ny * LANES

    def right_side(row, count):
        lane = lanes_of(count)
        at = lax.broadcasted_iota(jnp.int32, (count, LANES), 0) + (row - TOP[0] + gx * ROWS)
        flat = at * width + lane + gy * LANES
        middle = (lane >= 32) & (lane < 96)
        side = jnp.where(lane >= 64, lane - LANES, lane + LANES)
        side = jnp.where(middle, jnp.where(lane >= 64, lane + 64, lane - 64), side)
        flat_side = at * width + side + gy * LANES + jnp.where(middle, plane, 0)
        places = (flat, flat + plane, flat_side)
        for t in range(3):
            source = jnp.zeros((count, LANES), jnp.float32)
            for number in range(WELLS):
                source = source + jnp.where(places[t] == well_cells[0, number], well_rates[0, number], 0.0)
            rows = pl.ds(row, count)
            g0[t, rows, :] = e0[5, t, rows, :] * (accu[t, rows, :] * start[t, rows, :] + source)

    over(0, -32, 96, right_side)
    levels = ((e0, g0), (e1, g1), (e2, g2))
    spare = (va, vb, r0, ua, ub, r1, wa, wb)
    sweep(start, va, g0, e0, 0, -32, 96)
    vcycle(levels, spare, pv)

    loads[4].wait()
    for layer in range(2):
        ext2[layer, own, :] = pv[layer, own, :] - observed_v[layer]
    for half in range(2):
        rows = pl.ds(TOP[0] + 32 * half, 32)
        pack(ext2[0, rows, :], ext2[1, rows, :], to_west2, to_east2, (pl.ds(16 * half, 16), slice(None)))
    copies2 = exchange(ext2, to_west2, to_east2, from_west2, from_east2, send2, recv2)
    stores = [pltpu.make_async_copy(pv.at[0:2, own, :], pressure_out.at[0], store_sem.at[0])]
    stores[0].start()
    for copy in copies2:
        copy.wait_recv()
    for block in range(4):
        unpack(from_west2, from_east2, ext2.at[2], (pl.ds(16 * block, 16), slice(None)), GUARD + 32 * block)

    def adjoint_side(row, count):
        for t in range(3):
            rows = pl.ds(row, count)
            value = e0[5, t, rows, :] * ext2[t, rows, :]
            g0[t, rows, :] = value
            va[t, rows, :] = value

    over(0, -32, 96, adjoint_side)
    vcycle(levels, spare, vb)
    stores.append(pltpu.make_async_copy(vb.at[0:2, own, :], adjoint_out.at[0], store_sem.at[1]))
    stores[1].start()

    def gradient(row, count):
        lane = lanes_of(count)
        rows = pl.ds(row, count)
        before, after = pl.ds(row - 1, count), pl.ds(row + 1, count)
        p, a = tiles(pv, row, count), tiles(vb, row, count)
        pr = to_right(*p, turn(p[2], 64), turn(p[1], 64), lane, 1)
        ar = to_right(*a, turn(a[2], 64), turn(a[1], 64), lane, 1)
        ge = []
        for t in range(3):
            c = f0[0, t, rows, :]
            ge.append(c * c * (p[t] - pr[t]) * (a[t] - ar[t]))
        gw = to_left(*ge, turn(ge[2], 64), ge[1], lane, 1)
        c = f0[2, 0, rows, :]
        gv = c * c * (1.0 / VERTICAL) * (p[0] - p[1]) * (a[0] - a[1])
        for t in range(2):
            c = f0[1, t, rows, :]
            gs = c * c * (p[t] - pv[t, after, :]) * (a[t] - vb[t, after, :])
            c = f0[1, t, before, :]
            gn = c * c * (p[t] - pv[t, before, :]) * (a[t] - vb[t, before, :])
            total_faces = ((ge[t] + gw[t]) + (gs + gn)) + gv
            terms[me, t, pl.ds(row - TOP[0], count), :] = -0.5 * total_faces / perm[t, rows, :]

    copies3 = []
    for half in range(2):
        over(0, 32 * half, 32 * half + 32, gradient)
        part = terms.at[me, :, pl.ds(32 * half, 32), :]
        for k, target in enumerate(peers):
            copy = pltpu.make_async_remote_copy(
                src_ref=part, dst_ref=part, send_sem=send3.at[half, k], recv_sem=recv3.at[half, k],
                device_id=target, device_id_type=MESH,
            )
            copy.start()
            copies3.append(copy)
    for copy in copies3:
        copy.wait_recv()
    value = terms[0]
    for k in range(1, terms.shape[0]):
        value = value + terms[k]
    total[...] = value
    stores.append(pltpu.make_async_copy(total, gradient_out, store_sem.at[2]))
    stores[2].start()
    for copy in copies1 + copies2 + copies3:
        copy.wait_send()
    for copy in stores:
        copy.wait()


def shards(perm_log, facies, facies_scale, accumulation, previous, observed, well_cells, well_rates):
    ns = lax.axis_size("scen")
    f32 = jnp.float32
    block = (2, ROWS, LANES)
    anywhere = pl.BlockSpec(memory_space=pl.ANY)
    scalars = pl.BlockSpec(memory_space=pltpu.SMEM)

    def vmem(*shape):
        return pltpu.VMEM(shape, f32)

    level = [(3, HEIGHT[k], LANES) for k in range(3)]
    dma = pltpu.SemaphoreType.DMA
    scratch = [
        vmem(*block), pltpu.VMEM(block, jnp.int32), vmem(*block), vmem(3, *level[0]), vmem(*level[0]),
        vmem(3, 32, LANES), vmem(3, 32, LANES), vmem(3, 64, LANES), vmem(3, 64, LANES),
        vmem(32, LANES), vmem(32, LANES), vmem(64, LANES), vmem(64, LANES),
        *[vmem(4, *level[k]) for k in range(3)],
        *[vmem(7, *level[k]) for k in range(3)],
        *[vmem(*level[k]) for k in range(3)],
        *[vmem(*level[0]) for _ in range(3)],
        *[vmem(*level[1]) for _ in range(3)],
        *[vmem(*level[2]) for _ in range(2)],
        vmem(*level[0]), vmem(ns, *block), vmem(*block),
        dma((5,)), dma((3,)), dma((8,)), dma((8,)), dma((8,)), dma((8,)), dma((2, ns - 1)), dma((2, ns - 1)),
    ]
    return pl.pallas_call(
        kernel,
        out_shape=(
            jax.ShapeDtypeStruct((1, *block), f32),
            jax.ShapeDtypeStruct((1, *block), f32),
            jax.ShapeDtypeStruct(block, f32),
        ),
        in_specs=[anywhere, anywhere, scalars, anywhere, anywhere, anywhere, scalars, scalars],
        out_specs=(anywhere, anywhere, anywhere),
        scratch_shapes=scratch,
        compiler_params=pltpu.CompilerParams(
            collective_id=0, has_side_effects=True, vmem_limit_bytes=48 * 2**20
        ),
    )(perm_log, facies, facies_scale, accumulation, previous, observed, well_cells, well_rates)


def solution(mesh):
    return jax.shard_map(
        shards,
        mesh=mesh,
        in_specs=(
            P(None, "gx", "gy"),
            P(None, "gx", "gy"),
            P(),
            P(None, "gx", "gy"),
            P("scen", None, "gx", "gy"),
            P("scen", None, "gx", "gy"),
            P("scen", None),
            P("scen", None),
        ),
        out_specs=(P("scen", None, "gx", "gy"), P("scen", None, "gx", "gy"), P(None, "gx", "gy")),
        check_vma=False,
    )
```

```python
from functools import partial

import jax
import jax.numpy as jnp
from jax import lax
from jax.experimental import pallas as pl
from jax.experimental.pallas import tpu as pltpu
from jax.sharding import PartitionSpec as P

WELLS = 5
FACIES = 4
VERTICAL = 0.3
DAMPING = 0.8
ROWS = 64
LANES = 128
HALO = 32
GUARD = 8
VMEM = 62 * 2**20
MESH = pl.DeviceIdType.MESH

TOP = (GUARD + HALO, GUARD + HALO // 2, GUARD + HALO // 4)
HEIGHT = tuple(ROWS // 2**k + 2 * TOP[k] for k in range(3))
CHUNK = 128


def over(level, low, high, body, step=CHUNK):
    base = TOP[level]
    for row in range(low, high, step):
        body(base + row, min(step, high - row))


def lanes_of(count):
    return lax.broadcasted_iota(jnp.int32, (count, LANES), 1)


def turn(value, shift):
    return pltpu.roll(value, shift % LANES, 1)


def to_right(m0, m1, h, hs, m1s, lane, s):
    return (
        turn(jnp.where(lane < s, h, m0), -s),
        turn(jnp.where(lane < s, hs, m1), -s),
        turn(jnp.where(lane < s, m0, jnp.where((lane >= 64) & (lane < 64 + s), m1s, h)), -s),
    )


def to_left(m0, m1, h, hs, m1s, lane, s):
    return (
        turn(jnp.where(lane >= LANES - s, h, m0), s),
        turn(jnp.where(lane >= LANES - s, hs, m1), s),
        turn(jnp.where(lane >= LANES - s, m0, jnp.where((lane >= 64 - s) & (lane < 64), m1s, h)), s),
    )


def tiles(ref, row, count):
    return tuple(ref[t, pl.ds(row, count), :] for t in range(3))


def change(v, g, e, level, row, count):
    s = 2**level
    lane = lanes_of(count)
    m0, m1, h = tiles(v, row, count)
    hs, m1s = turn(h, 64), turn(m1, 64)
    right = to_right(m0, m1, h, hs, m1s, lane, s)
    left = to_left(m0, m1, h, hs, m1s, lane, s)
    across = (m1, m0, hs)
    up = tiles(v, row - 1, count)
    down = tiles(v, row + 1, count)
    mid = (m0, m1, h)
    rows = pl.ds(row, count)
    out = []
    for t in range(3):
        near = e[0, t, rows, :] * up[t] + e[1, t, rows, :] * down[t]
        side = e[2, t, rows, :] * right[t] + e[3, t, rows, :] * left[t]
        out.append(
            (near + side) + (e[4, t, rows, :] * across[t] + (g[t, rows, :] - DAMPING * mid[t]))
        )
    return out, mid


def sweep(v, out, g, e, level, low, high):
    def body(row, count):
        delta, mid = change(v, g, e, level, row, count)
        for t in range(3):
            out[t, pl.ds(row, count), :] = mid[t] + delta[t]

    over(level, low, high, body)


def residual(v, out, g, e, level, low, high):
    def body(row, count):
        delta, _ = change(v, g, e, level, row, count)
        for t in range(3):
            out[t, pl.ds(row, count), :] = delta[t] * e[6, t, pl.ds(row, count), :]

    over(level, low, high, body)


def pair_sum(value, lane, s):
    both = value + turn(value, -s)
    return jnp.where(lane % (2 * s) < s, both, turn(both, s))


def even_odd(ref, index, row, count):
    first = ref[(*index, pl.ds(row, count, stride=2), slice(None))]
    second = ref[(*index, pl.ds(row + 1, count, stride=2), slice(None))]
    return first, second


def restrict(fine, g, e, level, low, high):
    s = 2 ** (level - 1)

    def body(row, count):
        lane = lanes_of(count)
        source = TOP[level - 1] + 2 * (row - TOP[level])
        for t in range(3):
            first, second = even_odd(fine, (t,), source, count)
            g[t, pl.ds(row, count), :] = pair_sum(first + second, lane, s) * e[5, t, pl.ds(row, count), :]

    over(level, low, high, body)


def prolong(coarse, fine, level, low, high):
    def body(row, count):
        target = TOP[level - 1] + 2 * (row - TOP[level])
        for t in range(3):
            value = coarse[t, pl.ds(row, count), :]
            for k in range(2):
                rows = pl.ds(target + k, count, stride=2)
                fine[t, rows, :] = fine[t, rows, :] + value

    over(level, low, high, body)


def coarsen(fine, coarse, level, low, high):
    s = 2 ** (level - 1)

    def body(row, count):
        lane = lanes_of(count)
        source = TOP[level - 1] + 2 * (row - TOP[level])
        rows = pl.ds(row, count)
        for t in range(3):
            first, second = even_odd(fine, (0, t), source, count)
            total = first + second
            coarse[0, t, rows, :] = jnp.where(lane % (2 * s) < s, turn(total, -s), total)
            second = fine[1, t, pl.ds(source + 1, count, stride=2), :]
            coarse[1, t, rows, :] = pair_sum(second, lane, s)
            for k in (2, 3):
                first, second = even_odd(fine, (k, t), source, count)
                coarse[k, t, rows, :] = pair_sum(first + second, lane, s)

    over(level, low, high, body)


def scale(faces, e, level, low, high):
    s = 2**level

    def body(row, count):
        lane = lanes_of(count)
        rows = pl.ds(row, count)
        east = tiles(faces.at[0], row, count)
        west = to_left(*east, turn(east[2], 64), turn(east[1], 64), lane, s)
        for t in range(3):
            south = faces[1, t, rows, :]
            north = faces[1, t, pl.ds(row - 1, count), :]
            across = faces[2, t, rows, :]
            diag = ((north + south) + (east[t] + west[t])) + (across + faces[3, t, rows, :])
            w = DAMPING / diag
            e[0, t, rows, :] = w * north
            e[1, t, rows, :] = w * south
            e[2, t, rows, :] = w * east[t]
            e[3, t, rows, :] = w * west[t]
            e[4, t, rows, :] = w * across
            e[5, t, rows, :] = w
            e[6, t, rows, :] = diag * (1.0 / DAMPING)

    over(level, low, high, body)


def harmonic(left, right):
    return 2.0 * left * right / (left + right)


def fine_faces(perm, faces, gx, gy, nx, ny, low, high):
    def body(row, count):
        lane = lanes_of(count)
        at = lax.broadcasted_iota(jnp.int32, (count, LANES), 0) + (row - TOP[0])
        m0, m1, h = tiles(perm, row, count)
        hs, m1s = turn(h, 64), turn(m1, 64)
        right = to_right(m0, m1, h, hs, m1s, lane, 1)
        below = tiles(perm, row + 1, count)
        wall = ((at == -1) & (gx == 0)) | ((at == ROWS - 1) & (gx == nx - 1))
        east = (lane == LANES - 1) & (gy == ny - 1)
        west = ((lane == LANES - 1) | (lane == 63)) & (gy == 0)
        own = (m0, m1, h)
        for t in range(3):
            edge = west if t == 2 else east
            faces[0, t, pl.ds(row, count), :] = jnp.where(edge, 0.0, harmonic(own[t], right[t]))
            faces[1, t, pl.ds(row, count), :] = jnp.where(wall, 0.0, harmonic(own[t], below[t]))
        between = VERTICAL * harmonic(m0, m1)
        faces[2, 0, pl.ds(row, count), :] = between
        faces[2, 1, pl.ds(row, count), :] = between
        faces[2, 2, pl.ds(row, count), :] = VERTICAL * harmonic(h, hs)

    over(0, low, high, body)


def vcycle(levels, spare, last):
    (e0, g0), (e1, g1), (e2, g2) = levels
    va, vb, r0, ua, ub, r1, wa, wb = spare
    sweep(va, vb, g0, e0, 0, -32, 96)
    residual(vb, r0, g0, e0, 0, -24, 88)
    restrict(r0, g1, e1, 1, -16, 48)
    sweep(g1, ub, g1, e1, 1, -16, 48)
    residual(ub, r1, g1, e1, 1, -16, 48)
    restrict(r1, g2, e2, 2, -8, 24)
    sweep(g2, wa, g2, e2, 2, -8, 24)
    sweep(wa, wb, g2, e2, 2, -8, 24)
    sweep(wb, wa, g2, e2, 2, -8, 24)
    prolong(wa, ub, 2, -4, 20)
    sweep(ub, ua, g1, e1, 1, -8, 40)
    sweep(ua, ub, g1, e1, 1, -8, 40)
    prolong(ub, vb, 1, -8, 40)
    sweep(vb, va, g0, e0, 0, -8, 72)
    sweep(va, last, g0, e0, 0, -8, 72)


def pack(m0, m1, to_west, to_east, index):
    lane = lanes_of(32)
    m1s = turn(m1, 64)
    outer = lane % 64 < 32
    for source, target, keep in (
        (jnp.where(lane < 64, m0, m1s), to_west, outer),
        (jnp.where(lane < 64, m1s, m0), to_east, jnp.logical_not(outer)),
    ):
        target[index] = jnp.where(keep[:16], source[:16], turn(source[16:], 32))


def unpack(from_west, from_east, target, source_index, row):
    outer = lanes_of(16) % 64 < 32
    west, east = from_west[source_index], from_east[source_index]
    target[pl.ds(row, 16), :] = jnp.where(outer, east, west)
    target[pl.ds(row + 16, 16), :] = turn(jnp.where(outer, west, east), -32)


def kernel(
    perm_log, facies, scale_in, accumulation, previous, observed, cells_in, rates_in,
    pressure_out, adjoint_out, gradient_out,
    facies_scale, well_cells, well_rates, log_v, facies_v, observed_v, ext, ext2, to_west, to_east, from_west, from_east,
    to_west2, to_east2, from_west2, from_east2,
    f0, f1, f2, e0, e1, e2, g0, g1, g2, va, vb, r0, ua, ub, r1, wa, wb, pv, terms,
    load_sem, send1, recv1, send2, recv2, send3, recv3,
):
    nx, ny, ns = lax.axis_size("gx"), lax.axis_size("gy"), lax.axis_size("scen")
    gx, gy, me = lax.axis_index("gx"), lax.axis_index("gy"), lax.axis_index("scen")
    north, south = lax.rem(gx + nx - 1, nx), lax.rem(gx + 1, nx)
    west, east = lax.rem(gy + ny - 1, ny), lax.rem(gy + 1, ny)
    around = [
        {"gx": north}, {"gx": south}, {"gy": west}, {"gy": east},
        {"gx": north, "gy": west}, {"gx": north, "gy": east},
        {"gx": south, "gy": west}, {"gx": south, "gy": east},
    ]
    peers = [{"scen": lax.rem(me + k, ns)} for k in range(1, ns)]

    own = pl.ds(TOP[0], ROWS)
    loads = [
        pltpu.make_async_copy(perm_log, log_v, load_sem.at[0]),
        pltpu.make_async_copy(facies, facies_v, load_sem.at[1]),
        pltpu.make_async_copy(accumulation, ext.at[1, 0:2, own, :], load_sem.at[2]),
        pltpu.make_async_copy(previous.at[0], ext.at[2, 0:2, own, :], load_sem.at[3]),
        pltpu.make_async_copy(scale_in, facies_scale, load_sem.at[4]),
        pltpu.make_async_copy(cells_in, well_cells, load_sem.at[5]),
        pltpu.make_async_copy(rates_in, well_rates, load_sem.at[6]),
        pltpu.make_async_copy(observed.at[0], observed_v, load_sem.at[7]),
    ]
    for copy in loads:
        copy.start()
    barrier = pltpu.get_barrier_semaphore()
    for target in around + peers:
        pl.semaphore_signal(barrier, inc=1, device_id=target, device_id_type=MESH)

    for copy in loads[:7]:
        copy.wait()
    for layer in range(2):
        labels = facies_v[layer]
        factor = jnp.zeros((ROWS, LANES), jnp.float32)
        for label in range(FACIES):
            factor = jnp.where(labels == label, facies_scale[label], factor)
        ext[0, layer, own, :] = jnp.exp(log_v[layer]) * factor
    for field in range(3):
        for half in range(2):
            rows = pl.ds(TOP[0] + 32 * half, 32)
            pack(ext[field, 0, rows, :], ext[field, 1, rows, :], to_west, to_east, (field, pl.ds(16 * half, 16), slice(None)))
    pl.semaphore_wait(barrier, len(around) + len(peers))

    def exchange(block, w_out, e_out, w_in, e_in, send, recv):
        upper, lower = pl.ds(TOP[0], HALO), pl.ds(TOP[0] + ROWS - HALO, HALO)
        above, below = pl.ds(GUARD, HALO), pl.ds(TOP[0] + ROWS, HALO)
        first, second = pl.ds(0, 16), pl.ds(16, 16)
        lead = (slice(None),) * (len(w_out.shape) - 2)
        pairs = [
            (block.at[(*lead, slice(0, 2), upper)], block.at[(*lead, slice(0, 2), below)]),
            (block.at[(*lead, slice(0, 2), lower)], block.at[(*lead, slice(0, 2), above)]),
            (w_out, e_in.at[(*lead, pl.ds(16, 32))]),
            (e_out, w_in.at[(*lead, pl.ds(16, 32))]),
            (w_out.at[(*lead, first)], e_in.at[(*lead, pl.ds(48, 16))]),
            (e_out.at[(*lead, first)], w_in.at[(*lead, pl.ds(48, 16))]),
            (w_out.at[(*lead, second)], e_in.at[(*lead, pl.ds(0, 16))]),
            (e_out.at[(*lead, second)], w_in.at[(*lead, pl.ds(0, 16))]),
        ]
        copies = [
            pltpu.make_async_remote_copy(
                src_ref=source, dst_ref=target, send_sem=send.at[k], recv_sem=recv.at[k],
                device_id=around[k], device_id_type=MESH,
            )
            for k, (source, target) in enumerate(pairs)
        ]
        for k in (4, 5, 6, 7, 2, 3, 0, 1):
            copies[k].start()
        return copies

    copies1 = exchange(ext, to_west, to_east, from_west, from_east, send1, recv1)
    for copy in copies1:
        copy.wait_recv()
    for field in range(3):
        for block in range(4):
            unpack(from_west, from_east, ext.at[field, 2], (field, pl.ds(16 * block, 16), slice(None)), GUARD + 32 * block)

    perm, accu, start = ext.at[0], ext.at[1], ext.at[2]
    fine_faces(perm, f0, gx, gy, nx, ny, -32, 96)

    def keep_accumulation(row, count):
        for t in range(3):
            f0[3, t, pl.ds(row, count), :] = accu[t, pl.ds(row, count), :]

    over(0, -32, 96, keep_accumulation)
    coarsen(f0, f1, 1, -16, 48)
    coarsen(f1, f2, 2, -8, 24)
    scale(f0, e0, 0, -32, 96)
    scale(f1, e1, 1, -16, 48)
    scale(f2, e2, 2, -8, 24)

    plane, width = nx * ROWS * ny * LANES, ny * LANES

    def right_side(row, count):
        lane = lanes_of(count)
        at = lax.broadcasted_iota(jnp.int32, (count, LANES), 0) + (row - TOP[0] + gx * ROWS)
        flat = at * width + lane + gy * LANES
        middle = (lane >= 32) & (lane < 96)
        side = jnp.where(lane >= 64, lane - LANES, lane + LANES)
        side = jnp.where(middle, jnp.where(lane >= 64, lane + 64, lane - 64), side)
        flat_side = at * width + side + gy * LANES + jnp.where(middle, plane, 0)
        places = (flat, flat + plane, flat_side)
        for t in range(3):
            source = jnp.zeros((count, LANES), jnp.float32)
            for number in range(WELLS):
                source = source + jnp.where(places[t] == well_cells[0, number], well_rates[0, number], 0.0)
            rows = pl.ds(row, count)
            g0[t, rows, :] = e0[5, t, rows, :] * (accu[t, rows, :] * start[t, rows, :] + source)

    over(0, -32, 96, right_side)
    levels = ((e0, g0), (e1, g1), (e2, g2))
    spare = (va, vb, r0, ua, ub, r1, wa, wb)
    sweep(start, va, g0, e0, 0, -32, 96)
    vcycle(levels, spare, pv)

    loads[7].wait()
    for layer in range(2):
        ext2[layer, own, :] = pv[layer, own, :] - observed_v[layer]
    for half in range(2):
        rows = pl.ds(TOP[0] + 32 * half, 32)
        pack(ext2[0, rows, :], ext2[1, rows, :], to_west2, to_east2, (pl.ds(16 * half, 16), slice(None)))
    copies2 = exchange(ext2, to_west2, to_east2, from_west2, from_east2, send2, recv2)
    pressure_out[0] = pv[0:2, own, :]
    for copy in copies2:
        copy.wait_recv()
    for block in range(4):
        unpack(from_west2, from_east2, ext2.at[2], (pl.ds(16 * block, 16), slice(None)), GUARD + 32 * block)

    def adjoint_side(row, count):
        for t in range(3):
            rows = pl.ds(row, count)
            value = e0[5, t, rows, :] * ext2[t, rows, :]
            g0[t, rows, :] = value
            va[t, rows, :] = value

    over(0, -32, 96, adjoint_side)
    vcycle(levels, spare, vb)
    adjoint_out[0] = vb[0:2, own, :]

    def gradient(row, count):
        lane = lanes_of(count)
        rows = pl.ds(row, count)
        before, after = pl.ds(row - 1, count), pl.ds(row + 1, count)
        p, a = tiles(pv, row, count), tiles(vb, row, count)
        pr = to_right(*p, turn(p[2], 64), turn(p[1], 64), lane, 1)
        ar = to_right(*a, turn(a[2], 64), turn(a[1], 64), lane, 1)
        ge = []
        for t in range(3):
            c = f0[0, t, rows, :]
            ge.append(c * c * (p[t] - pr[t]) * (a[t] - ar[t]))
        gw = to_left(*ge, turn(ge[2], 64), ge[1], lane, 1)
        c = f0[2, 0, rows, :]
        gv = c * c * (1.0 / VERTICAL) * (p[0] - p[1]) * (a[0] - a[1])
        for t in range(2):
            c = f0[1, t, rows, :]
            gs = c * c * (p[t] - pv[t, after, :]) * (a[t] - vb[t, after, :])
            c = f0[1, t, before, :]
            gn = c * c * (p[t] - pv[t, before, :]) * (a[t] - vb[t, before, :])
            total_faces = ((ge[t] + gw[t]) + (gs + gn)) + gv
            terms[me, t, pl.ds(row - TOP[0], count), :] = -0.5 * total_faces / perm[t, rows, :]

    copies3 = []
    for half in range(2):
        over(0, 32 * half, 32 * half + 32, gradient)
        part = terms.at[me, :, pl.ds(32 * half, 32), :]
        for k, target in enumerate(peers):
            copy = pltpu.make_async_remote_copy(
                src_ref=part, dst_ref=part, send_sem=send3.at[half, k], recv_sem=recv3.at[half, k],
                device_id=target, device_id_type=MESH,
            )
            copy.start()
            copies3.append(copy)
    for copy in copies3:
        copy.wait_recv()
    value = terms[0]
    for k in range(1, terms.shape[0]):
        value = value + terms[k]
    gradient_out[...] = value
    for copy in copies1 + copies2 + copies3:
        copy.wait_send()


def store(*refs):
    sem = refs[-1]
    copies = [pltpu.make_async_copy(refs[k], refs[k + 3], sem.at[k]) for k in range(3)]
    for copy in copies:
        copy.start()
    for copy in copies:
        copy.wait()


def shards(perm_log, facies, facies_scale, accumulation, previous, observed, well_cells, well_rates):
    ns = lax.axis_size("scen")
    f32 = jnp.float32
    block = (2, ROWS, LANES)
    anywhere = pl.BlockSpec(memory_space=pl.ANY)

    def vmem(*shape):
        return pltpu.VMEM(shape, f32)

    level = [(3, HEIGHT[k], LANES) for k in range(3)]
    dma = pltpu.SemaphoreType.DMA
    scratch = [
        pltpu.SMEM((FACIES,), f32), pltpu.SMEM((1, WELLS), jnp.int32), pltpu.SMEM((1, WELLS), f32),
        vmem(*block), pltpu.VMEM(block, jnp.int32), vmem(*block), vmem(3, *level[0]), vmem(*level[0]),
        vmem(3, 32, LANES), vmem(3, 32, LANES), vmem(3, 64, LANES), vmem(3, 64, LANES),
        vmem(32, LANES), vmem(32, LANES), vmem(64, LANES), vmem(64, LANES),
        *[vmem(4, *level[k]) for k in range(3)],
        *[vmem(7, *level[k]) for k in range(3)],
        *[vmem(*level[k]) for k in range(3)],
        *[vmem(*level[0]) for _ in range(3)],
        *[vmem(*level[1]) for _ in range(3)],
        *[vmem(*level[2]) for _ in range(2)],
        vmem(*level[0]), vmem(ns, *block),
        dma((8,)), dma((8,)), dma((8,)), dma((8,)), dma((8,)), dma((2, ns - 1)), dma((2, ns - 1)),
    ]
    shapes = ((1, *block), (1, *block), block)
    results = pl.pallas_call(
        kernel,
        out_shape=tuple(vmem(*shape) for shape in shapes),
        in_specs=[anywhere] * 8,
        out_specs=(pl.BlockSpec(memory_space=pltpu.VMEM),) * 3,
        scratch_shapes=scratch,
        compiler_params=pltpu.CompilerParams(
            collective_id=0, has_side_effects=True, vmem_limit_bytes=VMEM
        ),
    )(perm_log, facies, facies_scale, accumulation, previous, observed, well_cells, well_rates)
    return pl.pallas_call(
        store,
        out_shape=tuple(jax.ShapeDtypeStruct(shape, f32) for shape in shapes),
        in_specs=[anywhere] * 3,
        out_specs=(anywhere,) * 3,
        scratch_shapes=[dma((3,))],
        compiler_params=pltpu.CompilerParams(vmem_limit_bytes=2**20),
    )(*results)


def solution(mesh):
    return jax.shard_map(
        shards,
        mesh=mesh,
        in_specs=(
            P(None, "gx", "gy"),
            P(None, "gx", "gy"),
            P(),
            P(None, "gx", "gy"),
            P("scen", None, "gx", "gy"),
            P("scen", None, "gx", "gy"),
            P("scen", None),
            P("scen", None),
        ),
        out_specs=(P("scen", None, "gx", "gy"), P("scen", None, "gx", "gy"), P(None, "gx", "gy")),
        check_vma=False,
    )
```

```python
import jax
import jax.numpy as jnp
from jax import lax
from jax.experimental import pallas as pl
from jax.experimental.pallas import tpu as pltpu
from jax.sharding import PartitionSpec as P

WELLS = 5
FACIES = 4
VERTICAL = 0.3
DAMPING = 0.8
ROWS = 64
LANES = 128
HALO = 32
GUARD = 8
VMEM = 62 * 2**20
MESH = pl.DeviceIdType.MESH

TOP = (GUARD + HALO, GUARD + HALO // 2, GUARD + HALO // 4)
HEIGHT = tuple(ROWS // 2**k + 2 * TOP[k] for k in range(3))
CHUNK = 8
TILES = 4


def over(level, low, high, body, step=CHUNK):
    base = TOP[level]
    for row in range(low, high, step):
        body(base + row, min(step, high - row))


def lanes_of(count):
    return lax.broadcasted_iota(jnp.int32, (count, LANES), 1)


def turn(value, shift):
    return pltpu.roll(value, shift % LANES, 1)


def to_right(values, lane, s):
    wrapped = lane < s
    return [turn(jnp.where(wrapped, values[t ^ 2], values[t]), -s) for t in range(TILES)]


def to_left(values, lane, s):
    wrapped = lane >= LANES - s
    return [turn(jnp.where(wrapped, values[t ^ 2], values[t]), s) for t in range(TILES)]


def tiles(ref, row, count):
    return [ref[t, pl.ds(row, count), :] for t in range(TILES)]


def change(v, g, e, level, row, count):
    s = 2**level
    lane = lanes_of(count)
    mid = tiles(v, row, count)
    right, left = to_right(mid, lane, s), to_left(mid, lane, s)
    up = tiles(v, row - 1, count)
    down = tiles(v, row + 1, count)
    rows = pl.ds(row, count)
    out = []
    for t in range(TILES):
        near = e[0, t, rows, :] * up[t] + e[1, t, rows, :] * down[t]
        side = e[2, t, rows, :] * right[t] + e[3, t, rows, :] * left[t]
        out.append(
            (near + side) + (e[4, t, rows, :] * mid[t ^ 1] + (g[t, rows, :] - DAMPING * mid[t]))
        )
    return out, mid


def sweep(v, out, g, e, level, low, high):
    def body(row, count):
        delta, mid = change(v, g, e, level, row, count)
        for t in range(TILES):
            out[t, pl.ds(row, count), :] = mid[t] + delta[t]

    over(level, low, high, body)


def residual(v, out, g, e, level, low, high):
    def body(row, count):
        delta, _ = change(v, g, e, level, row, count)
        for t in range(TILES):
            out[t, pl.ds(row, count), :] = delta[t] * e[6, t, pl.ds(row, count), :]

    over(level, low, high, body)


def pair_sum(value, lane, s):
    return value + jnp.where(lane % (2 * s) < s, turn(value, -s), turn(value, s))


def even_odd(ref, index, row, count):
    first = ref[(*index, pl.ds(row, count, stride=2), slice(None))]
    second = ref[(*index, pl.ds(row + 1, count, stride=2), slice(None))]
    return first, second


def restrict(fine, g, e, level, low, high):
    s = 2 ** (level - 1)

    def body(row, count):
        lane = lanes_of(count)
        source = TOP[level - 1] + 2 * (row - TOP[level])
        for t in range(TILES):
            first, second = even_odd(fine, (t,), source, count)
            g[t, pl.ds(row, count), :] = pair_sum(first + second, lane, s) * e[5, t, pl.ds(row, count), :]

    over(level, low, high, body)


def prolong(coarse, fine, level, low, high):
    def body(row, count):
        target = TOP[level - 1] + 2 * (row - TOP[level])
        for t in range(TILES):
            value = coarse[t, pl.ds(row, count), :]
            for k in range(2):
                rows = pl.ds(target + k, count, stride=2)
                fine[t, rows, :] = fine[t, rows, :] + value

    over(level, low, high, body)


def coarsen(fine, coarse, level, low, high, members):
    s = 2 ** (level - 1)

    def body(row, count):
        lane = lanes_of(count)
        source = TOP[level - 1] + 2 * (row - TOP[level])
        rows = pl.ds(row, count)
        for k in members:
            for t in range(TILES):
                first, second = even_odd(fine, (k, t), source, count)
                if k == 0:
                    total = first + second
                    coarse[k, t, rows, :] = jnp.where(lane % (2 * s) < s, turn(total, -s), total)
                else:
                    coarse[k, t, rows, :] = pair_sum(second if k == 1 else first + second, lane, s)

    over(level, low, high, body)


def scale(faces, e, level, low, high):
    s = 2**level

    def body(row, count):
        lane = lanes_of(count)
        rows = pl.ds(row, count)
        east = tiles(faces.at[0], row, count)
        west = to_left(east, lane, s)
        for t in range(TILES):
            south = faces[1, t, rows, :]
            north = faces[1, t, pl.ds(row - 1, count), :]
            across = faces[2, t, rows, :]
            diag = ((north + south) + (east[t] + west[t])) + (across + faces[3, t, rows, :])
            w = DAMPING / diag
            e[0, t, rows, :] = w * north
            e[1, t, rows, :] = w * south
            e[2, t, rows, :] = w * east[t]
            e[3, t, rows, :] = w * west[t]
            e[4, t, rows, :] = w * across
            e[5, t, rows, :] = w
            e[6, t, rows, :] = diag * (1.0 / DAMPING)

    over(level, low, high, body)


def harmonic(left, right):
    return 2.0 * left * right / (left + right)


def fine_faces(perm, faces, gx, gy, nx, ny, low, high):
    def body(row, count):
        lane = lanes_of(count)
        at = lax.broadcasted_iota(jnp.int32, (count, LANES), 0) + (row - TOP[0])
        own = tiles(perm, row, count)
        right = to_right(own, lane, 1)
        below = tiles(perm, row + 1, count)
        wall = ((at == -1) & (gx == 0)) | ((at == ROWS - 1) & (gx == nx - 1))
        last = lane == LANES - 1
        edges = (last & (gy == ny - 1), last & (gy == 0))
        rows = pl.ds(row, count)
        for t in range(TILES):
            faces[0, t, rows, :] = jnp.where(edges[t // 2], 0.0, harmonic(own[t], right[t]))
            faces[1, t, rows, :] = jnp.where(wall, 0.0, harmonic(own[t], below[t]))
        for t in (0, 2):
            between = VERTICAL * harmonic(own[t], own[t + 1])
            faces[2, t, rows, :] = between
            faces[2, t + 1, rows, :] = between

    over(0, low, high, body)


def vcycle(levels, spare, last):
    (e0, g0), (e1, g1), (e2, g2) = levels
    va, vb, r0, ua, ub, r1, wa, wb = spare
    sweep(va, vb, g0, e0, 0, -32, 96)
    residual(vb, r0, g0, e0, 0, -24, 88)
    restrict(r0, g1, e1, 1, -16, 48)
    sweep(g1, ub, g1, e1, 1, -16, 48)
    residual(ub, r1, g1, e1, 1, -16, 48)
    restrict(r1, g2, e2, 2, -8, 24)
    sweep(g2, wa, g2, e2, 2, -8, 24)
    sweep(wa, wb, g2, e2, 2, -8, 24)
    sweep(wb, wa, g2, e2, 2, -8, 24)
    prolong(wa, ub, 2, -4, 20)
    sweep(ub, ua, g1, e1, 1, -8, 40)
    sweep(ua, ub, g1, e1, 1, -8, 40)
    prolong(ub, vb, 1, -8, 40)
    sweep(vb, va, g0, e0, 0, -8, 72)
    sweep(va, last, g0, e0, 0, -8, 72)


def pack(m0, m1, to_west, to_east, index):
    lane = lanes_of(16)
    outer = lane % 64 < 32
    first = lane < 64
    turned = (lane >= 32) & (lane < 96)
    upper = m0[:16], turn(m1[:16], 64)
    lower = turn(m0[16:], 32), turn(m1[16:], 96)
    for k, target in enumerate((to_west, to_east)):
        a = jnp.where(first, upper[k], upper[1 - k])
        b = jnp.where(turned, lower[k], lower[1 - k])
        target[index] = jnp.where(outer, a, b) if k == 0 else jnp.where(outer, b, a)


def unpack(from_west, from_east, block, index, row):
    outer = lanes_of(16) % 64 < 32
    west, east = from_west[index], from_east[index]
    upper, lower = jnp.where(outer, east, west), jnp.where(outer, west, east)
    block[2, pl.ds(row, 16), :] = upper
    block[3, pl.ds(row, 16), :] = turn(upper, 64)
    block[2, pl.ds(row + 16, 16), :] = turn(lower, -32)
    block[3, pl.ds(row + 16, 16), :] = turn(lower, 32)


def kernel(
    perm_log, facies, scale_in, accumulation, previous, observed, cells_in, rates_in,
    pressure_out, adjoint_out, gradient_out,
    facies_scale, well_cells, well_rates, log_v, facies_v, observed_v, ext, ext2, to_west, to_east, from_west, from_east,
    to_west2, to_east2, from_west2, from_east2,
    f0, f1, f2, e0, e1, e2, g0, g1, g2, va, vb, r0, ua, ub, r1, wa, wb, pv, q, terms,
    load_sem, send0, recv0, send1, recv1, send2, recv2, send3, recv3,
):
    nx, ny, ns = lax.axis_size("gx"), lax.axis_size("gy"), lax.axis_size("scen")
    gx, gy, me = lax.axis_index("gx"), lax.axis_index("gy"), lax.axis_index("scen")
    north, south = lax.rem(gx + nx - 1, nx), lax.rem(gx + 1, nx)
    west, east = lax.rem(gy + ny - 1, ny), lax.rem(gy + 1, ny)
    around = [
        {"gx": north}, {"gx": south}, {"gy": west}, {"gy": east},
        {"gx": north, "gy": west}, {"gx": north, "gy": east},
        {"gx": south, "gy": west}, {"gx": south, "gy": east},
    ]
    peers = [{"scen": lax.rem(me + k, ns)} for k in sorted(range(1, ns), key=lambda k: -min(k, ns - k))]

    own = pl.ds(TOP[0], ROWS)
    loads = [
        pltpu.make_async_copy(perm_log, log_v, load_sem.at[0]),
        pltpu.make_async_copy(facies, facies_v, load_sem.at[1]),
        pltpu.make_async_copy(accumulation, ext.at[1, 0:2, own, :], load_sem.at[2]),
        pltpu.make_async_copy(previous.at[0], ext.at[2, 0:2, own, :], load_sem.at[3]),
        pltpu.make_async_copy(scale_in, facies_scale, load_sem.at[4]),
        pltpu.make_async_copy(cells_in, well_cells, load_sem.at[5]),
        pltpu.make_async_copy(rates_in, well_rates, load_sem.at[6]),
        pltpu.make_async_copy(observed.at[0], observed_v, load_sem.at[7]),
    ]
    for copy in loads:
        copy.start()
    barrier = pltpu.get_barrier_semaphore()
    for target in around + peers:
        pl.semaphore_signal(barrier, inc=1, device_id=target, device_id_type=MESH)

    for copy in loads[:7]:
        copy.wait()
    for layer in range(2):
        labels = facies_v[layer]
        factor = jnp.zeros((ROWS, LANES), jnp.float32)
        for label in range(FACIES):
            factor = jnp.where(labels == label, facies_scale[label], factor)
        ext[0, layer, own, :] = jnp.exp(log_v[layer]) * factor
    for field in range(3):
        for half in range(2):
            rows = pl.ds(TOP[0] + 32 * half, 32)
            pack(ext[field, 0, rows, :], ext[field, 1, rows, :], to_west, to_east, (field, pl.ds(16 * half, 16), slice(None)))
    pl.semaphore_wait(barrier, len(around) + len(peers))

    def exchange(block, w_out, e_out, w_in, e_in, send, recv):
        upper, lower = pl.ds(TOP[0], HALO), pl.ds(TOP[0] + ROWS - HALO, HALO)
        above, below = pl.ds(GUARD, HALO), pl.ds(TOP[0] + ROWS, HALO)
        first, second = pl.ds(0, 16), pl.ds(16, 16)
        lead = (slice(None),) * (len(w_out.shape) - 2)
        pairs = [
            (block.at[(*lead, slice(0, 2), upper)], block.at[(*lead, slice(0, 2), below)]),
            (block.at[(*lead, slice(0, 2), lower)], block.at[(*lead, slice(0, 2), above)]),
            (w_out, e_in.at[(*lead, pl.ds(16, 32))]),
            (e_out, w_in.at[(*lead, pl.ds(16, 32))]),
            (w_out.at[(*lead, first)], e_in.at[(*lead, pl.ds(48, 16))]),
            (e_out.at[(*lead, first)], w_in.at[(*lead, pl.ds(48, 16))]),
            (w_out.at[(*lead, second)], e_in.at[(*lead, pl.ds(0, 16))]),
            (e_out.at[(*lead, second)], w_in.at[(*lead, pl.ds(0, 16))]),
        ]
        copies = [
            pltpu.make_async_remote_copy(
                src_ref=source, dst_ref=target, send_sem=send.at[k], recv_sem=recv.at[k],
                device_id=around[k], device_id_type=MESH,
            )
            for k, (source, target) in enumerate(pairs)
        ]
        for k in (4, 5, 6, 7, 2, 3, 0, 1):
            copies[k].start()
        return copies

    first, rest = pl.ds(0, 1), pl.ds(1, 2)
    copies0, copies1 = [
        exchange(*[ref.at[part] for ref in (ext, to_west, to_east, from_west, from_east)], send, recv)
        for part, send, recv in ((first, send0, recv0), (rest, send1, recv1))
    ]
    plane, width = nx * ROWS * ny * LANES, ny * LANES

    def sources(row, count):
        lane = lanes_of(count)
        at = lax.broadcasted_iota(jnp.int32, (count, LANES), 0) + (row - TOP[0] + gx * ROWS)
        flat = at * width + lane + gy * LANES
        side = flat + jnp.where(lane >= 64, -LANES, LANES)
        for t, place in enumerate((flat, flat + plane, side, side + plane)):
            source = jnp.zeros((count, LANES), jnp.float32)
            for number in range(WELLS):
                source = source + jnp.where(place == well_cells[0, number], well_rates[0, number], 0.0)
            g0[t, pl.ds(row, count), :] = source

    over(0, -32, 96, sources)

    def receive(copies, fields):
        for copy in copies:
            copy.wait_recv()
        for field in fields:
            for block in range(4):
                unpack(from_west, from_east, ext.at[field], (field, pl.ds(16 * block, 16), slice(None)), GUARD + 32 * block)

    receive(copies0, (0,))
    perm, accu, start = ext.at[0], ext.at[1], ext.at[2]
    fine_faces(perm, f0, gx, gy, nx, ny, -32, 96)
    coarsen(f0, f1, 1, -16, 48, (0, 1, 2))
    coarsen(f1, f2, 2, -8, 24, (0, 1, 2))
    receive(copies1, (1, 2))

    def right_side(row, count):
        rows = pl.ds(row, count)
        for t in range(TILES):
            value = accu[t, rows, :]
            f0[3, t, rows, :] = value
            g0[t, rows, :] = g0[t, rows, :] + value * start[t, rows, :]

    over(0, -32, 96, right_side)
    scale(f0, e0, 0, -32, 96)

    def weigh(row, count):
        rows = pl.ds(row, count)
        for t in range(TILES):
            g0[t, rows, :] = g0[t, rows, :] * e0[5, t, rows, :]

    over(0, -32, 96, weigh)
    coarsen(f0, f1, 1, -16, 48, (3,))
    coarsen(f1, f2, 2, -8, 24, (3,))
    scale(f1, e1, 1, -16, 48)
    scale(f2, e2, 2, -8, 24)
    levels = ((e0, g0), (e1, g1), (e2, g2))
    spare = (va, vb, r0, ua, ub, r1, wa, wb)
    sweep(start, va, g0, e0, 0, -32, 96)
    vcycle(levels, spare, pv)

    loads[7].wait()
    for layer in range(2):
        ext2[layer, own, :] = pv[layer, own, :] - observed_v[layer]
    for half in range(2):
        rows = pl.ds(TOP[0] + 32 * half, 32)
        pack(ext2[0, rows, :], ext2[1, rows, :], to_west2, to_east2, (pl.ds(16 * half, 16), slice(None)))
    copies2 = exchange(ext2, to_west2, to_east2, from_west2, from_east2, send2, recv2)
    pressure_out[0] = pv[0:2, own, :]

    def gradient_weights(row, count):
        lane = lanes_of(count)
        rows, before, after = pl.ds(row, count), pl.ds(row - 1, count), pl.ds(row + 1, count)
        p = tiles(pv, row, count)
        right, left = to_right(p, lane, 1), to_left(p, lane, 1)
        east = tiles(f0.at[0], row, count)
        west = to_left(east, lane, 1)
        for t in range(2):
            factor = -0.5 / perm[t, rows, :]
            south, north, across = f0[1, t, rows, :], f0[1, t, before, :], f0[2, t, rows, :]
            sides = (
                (north, pv[t, before, :], 1.0), (south, pv[t, after, :], 1.0), (east[t], right[t], 1.0),
                (west[t], left[t], 1.0), (across, p[t ^ 1], 1.0 / VERTICAL),
            )
            for k, (face, value, weight) in enumerate(sides):
                q[k, t, pl.ds(row - TOP[0], count), :] = factor * weight * (face * face) * (p[t] - value)

    over(0, 0, ROWS, gradient_weights)
    for copy in copies2:
        copy.wait_recv()
    for block in range(4):
        unpack(from_west2, from_east2, ext2, (pl.ds(16 * block, 16), slice(None)), GUARD + 32 * block)

    def adjoint_side(row, count):
        for t in range(TILES):
            rows = pl.ds(row, count)
            value = e0[5, t, rows, :] * ext2[t, rows, :]
            g0[t, rows, :] = value
            va[t, rows, :] = value

    over(0, -32, 96, adjoint_side)
    vcycle(levels, spare, vb)
    adjoint_out[0] = vb[0:2, own, :]

    def gradient(row, count):
        lane = lanes_of(count)
        before, after = pl.ds(row - 1, count), pl.ds(row + 1, count)
        a = tiles(vb, row, count)
        right, left = to_right(a, lane, 1), to_left(a, lane, 1)
        rows = pl.ds(row - TOP[0], count)
        for t in range(2):
            near = q[0, t, rows, :] * (a[t] - vb[t, before, :]) + q[1, t, rows, :] * (a[t] - vb[t, after, :])
            side = q[2, t, rows, :] * (a[t] - right[t]) + q[3, t, rows, :] * (a[t] - left[t])
            terms[me, t, rows, :] = (near + side) + q[4, t, rows, :] * (a[t] - a[t ^ 1])

    copies3 = []
    for half in range(2):
        over(0, 32 * half, 32 * half + 32, gradient)
        part = terms.at[me, :, pl.ds(32 * half, 32), :]
        for k, target in enumerate(peers):
            copy = pltpu.make_async_remote_copy(
                src_ref=part, dst_ref=part, send_sem=send3.at[half, k], recv_sem=recv3.at[half, k],
                device_id=target, device_id_type=MESH,
            )
            copy.start()
            copies3.append(copy)
    for copy in copies3:
        copy.wait_recv()
    value = terms[0]
    for k in range(1, terms.shape[0]):
        value = value + terms[k]
    gradient_out[...] = value
    for copy in copies0 + copies1 + copies2 + copies3:
        copy.wait_send()


def store(*refs):
    sem = refs[-1]
    copies = [pltpu.make_async_copy(refs[k], refs[k + 3], sem.at[k]) for k in range(3)]
    for copy in copies:
        copy.start()
    for copy in copies:
        copy.wait()


def shards(perm_log, facies, facies_scale, accumulation, previous, observed, well_cells, well_rates):
    ns = lax.axis_size("scen")
    f32 = jnp.float32
    block = (2, ROWS, LANES)
    anywhere = pl.BlockSpec(memory_space=pl.ANY)

    def vmem(*shape):
        return pltpu.VMEM(shape, f32)

    level = [(TILES, HEIGHT[k], LANES) for k in range(3)]
    dma = pltpu.SemaphoreType.DMA
    scratch = [
        pltpu.SMEM((FACIES,), f32), pltpu.SMEM((1, WELLS), jnp.int32), pltpu.SMEM((1, WELLS), f32),
        vmem(*block), pltpu.VMEM(block, jnp.int32), vmem(*block), vmem(3, *level[0]), vmem(*level[0]),
        vmem(3, 32, LANES), vmem(3, 32, LANES), vmem(3, 64, LANES), vmem(3, 64, LANES),
        vmem(32, LANES), vmem(32, LANES), vmem(64, LANES), vmem(64, LANES),
        *[vmem(4, *level[k]) for k in range(3)],
        *[vmem(7, *level[k]) for k in range(3)],
        *[vmem(*level[k]) for k in range(3)],
        *[vmem(*level[0]) for _ in range(3)],
        *[vmem(*level[1]) for _ in range(3)],
        *[vmem(*level[2]) for _ in range(2)],
        vmem(*level[0]), vmem(5, *block), vmem(ns, *block),
        *[dma((8,)) for _ in range(7)], dma((2, ns - 1)), dma((2, ns - 1)),
    ]
    shapes = ((1, *block), (1, *block), block)
    results = pl.pallas_call(
        kernel,
        out_shape=tuple(vmem(*shape) for shape in shapes),
        in_specs=[anywhere] * 8,
        out_specs=(pl.BlockSpec(memory_space=pltpu.VMEM),) * 3,
        scratch_shapes=scratch,
        compiler_params=pltpu.CompilerParams(
            collective_id=0, has_side_effects=True, vmem_limit_bytes=VMEM
        ),
    )(perm_log, facies, facies_scale, accumulation, previous, observed, well_cells, well_rates)
    return pl.pallas_call(
        store,
        out_shape=tuple(jax.ShapeDtypeStruct(shape, f32) for shape in shapes),
        in_specs=[anywhere] * 3,
        out_specs=(anywhere,) * 3,
        scratch_shapes=[dma((3,))],
        compiler_params=pltpu.CompilerParams(vmem_limit_bytes=2**20),
    )(*results)


def solution(mesh):
    return jax.shard_map(
        shards,
        mesh=mesh,
        in_specs=(
            P(None, "gx", "gy"),
            P(None, "gx", "gy"),
            P(),
            P(None, "gx", "gy"),
            P("scen", None, "gx", "gy"),
            P("scen", None, "gx", "gy"),
            P("scen", None),
            P("scen", None),
        ),
        out_specs=(P("scen", None, "gx", "gy"), P("scen", None, "gx", "gy"), P(None, "gx", "gy")),
        check_vma=False,
    )
```

```python
import jax
import jax.numpy as jnp
from jax import lax
from jax.experimental import pallas as pl
from jax.experimental.pallas import tpu as pltpu
from jax.sharding import PartitionSpec as P

WELLS = 5
FACIES = 4
VERTICAL = 0.3
DAMPING = 0.8
ROWS = 64
LANES = 128
HALO = 32
GUARD = 8
VMEM = 62 * 2**20
MESH = pl.DeviceIdType.MESH

TOP = (GUARD + HALO, GUARD + HALO // 2, GUARD + HALO // 4)
HEIGHT = tuple(ROWS // 2**k + 2 * TOP[k] for k in range(3))
CHUNK = 8
TILES = 4


def over(level, low, high, body, step=CHUNK):
    base = TOP[level]
    for row in range(low, high, step):
        body(base + row, min(step, high - row))


def lanes_of(count):
    return lax.broadcasted_iota(jnp.int32, (count, LANES), 1)


def turn(value, shift):
    return pltpu.roll(value, shift % LANES, 1)


def to_right(values, lane, s):
    wrapped = lane < s
    return [turn(jnp.where(wrapped, values[t ^ 2], values[t]), -s) for t in range(TILES)]


def to_left(values, lane, s):
    wrapped = lane >= LANES - s
    return [turn(jnp.where(wrapped, values[t ^ 2], values[t]), s) for t in range(TILES)]


def tiles(ref, row, count):
    return [ref[t, pl.ds(row, count), :] for t in range(TILES)]


def change(v, g, e, level, row, count):
    s = 2**level
    lane = lanes_of(count)
    mid = tiles(v, row, count)
    right, left = to_right(mid, lane, s), to_left(mid, lane, s)
    up = tiles(v, row - 1, count)
    down = tiles(v, row + 1, count)
    rows = pl.ds(row, count)
    out = []
    for t in range(TILES):
        near = e[0, t, rows, :] * up[t] + e[1, t, rows, :] * down[t]
        side = e[2, t, rows, :] * right[t] + e[3, t, rows, :] * left[t]
        out.append(
            (near + side) + (e[4, t, rows, :] * mid[t ^ 1] + (g[t, rows, :] - DAMPING * mid[t]))
        )
    return out, mid


def sweep(v, out, g, e, level, low, high):
    def body(row, count):
        delta, mid = change(v, g, e, level, row, count)
        for t in range(TILES):
            out[t, pl.ds(row, count), :] = mid[t] + delta[t]

    over(level, low, high, body)


def residual(v, out, g, e, level, low, high):
    def body(row, count):
        delta, _ = change(v, g, e, level, row, count)
        for t in range(TILES):
            out[t, pl.ds(row, count), :] = delta[t] * e[6, t, pl.ds(row, count), :]

    over(level, low, high, body)


def pair_sum(value, lane, s):
    return value + jnp.where(lane % (2 * s) < s, turn(value, -s), turn(value, s))


def even_odd(ref, index, row, count):
    first = ref[(*index, pl.ds(row, count, stride=2), slice(None))]
    second = ref[(*index, pl.ds(row + 1, count, stride=2), slice(None))]
    return first, second


def restrict(fine, g, e, level, low, high):
    s = 2 ** (level - 1)

    def body(row, count):
        lane = lanes_of(count)
        source = TOP[level - 1] + 2 * (row - TOP[level])
        for t in range(TILES):
            first, second = even_odd(fine, (t,), source, count)
            g[t, pl.ds(row, count), :] = pair_sum(first + second, lane, s) * e[5, t, pl.ds(row, count), :]

    over(level, low, high, body)


def prolong(coarse, fine, level, low, high):
    def body(row, count):
        target = TOP[level - 1] + 2 * (row - TOP[level])
        for t in range(TILES):
            value = coarse[t, pl.ds(row, count), :]
            for k in range(2):
                rows = pl.ds(target + k, count, stride=2)
                fine[t, rows, :] = fine[t, rows, :] + value

    over(level, low, high, body)


def coarsen(fine, coarse, level, low, high, members):
    s = 2 ** (level - 1)

    def body(row, count):
        lane = lanes_of(count)
        source = TOP[level - 1] + 2 * (row - TOP[level])
        rows = pl.ds(row, count)
        for k in members:
            for t in range(TILES):
                first, second = even_odd(fine, (k, t), source, count)
                if k == 0:
                    total = first + second
                    coarse[k, t, rows, :] = jnp.where(lane % (2 * s) < s, turn(total, -s), total)
                else:
                    coarse[k, t, rows, :] = pair_sum(second if k == 1 else first + second, lane, s)

    over(level, low, high, body)


def scale(faces, e, level, low, high):
    s = 2**level

    def body(row, count):
        lane = lanes_of(count)
        rows = pl.ds(row, count)
        east = tiles(faces.at[0], row, count)
        west = to_left(east, lane, s)
        for t in range(TILES):
            south = faces[1, t, rows, :]
            north = faces[1, t, pl.ds(row - 1, count), :]
            across = faces[2, t, rows, :]
            diag = ((north + south) + (east[t] + west[t])) + (across + faces[3, t, rows, :])
            w = DAMPING / diag
            e[0, t, rows, :] = w * north
            e[1, t, rows, :] = w * south
            e[2, t, rows, :] = w * east[t]
            e[3, t, rows, :] = w * west[t]
            e[4, t, rows, :] = w * across
            e[5, t, rows, :] = w
            e[6, t, rows, :] = diag * (1.0 / DAMPING)

    over(level, low, high, body)


def harmonic(left, right):
    return 2.0 * left * right / (left + right)


def fine_faces(perm, faces, gx, gy, nx, ny, low, high):
    def body(row, count):
        lane = lanes_of(count)
        at = lax.broadcasted_iota(jnp.int32, (count, LANES), 0) + (row - TOP[0])
        own = tiles(perm, row, count)
        right = to_right(own, lane, 1)
        below = tiles(perm, row + 1, count)
        wall = ((at == -1) & (gx == 0)) | ((at == ROWS - 1) & (gx == nx - 1))
        last = lane == LANES - 1
        edges = (last & (gy == ny - 1), last & (gy == 0))
        rows = pl.ds(row, count)
        for t in range(TILES):
            faces[0, t, rows, :] = jnp.where(edges[t // 2], 0.0, harmonic(own[t], right[t]))
            faces[1, t, rows, :] = jnp.where(wall, 0.0, harmonic(own[t], below[t]))
        for t in (0, 2):
            between = VERTICAL * harmonic(own[t], own[t + 1])
            faces[2, t, rows, :] = between
            faces[2, t + 1, rows, :] = between

    over(0, low, high, body)


def vcycle(levels, spare, last):
    (e0, g0), (e1, g1), (e2, g2) = levels
    va, vb, r0, ua, ub, r1, wa, wb = spare
    sweep(va, vb, g0, e0, 0, -32, 96)
    residual(vb, r0, g0, e0, 0, -24, 88)
    restrict(r0, g1, e1, 1, -16, 48)
    sweep(g1, ub, g1, e1, 1, -16, 48)
    residual(ub, r1, g1, e1, 1, -16, 48)
    restrict(r1, g2, e2, 2, -8, 24)
    sweep(g2, wa, g2, e2, 2, -8, 24)
    sweep(wa, wb, g2, e2, 2, -8, 24)
    sweep(wb, wa, g2, e2, 2, -8, 24)
    prolong(wa, ub, 2, -4, 20)
    sweep(ub, ua, g1, e1, 1, -8, 40)
    sweep(ua, ub, g1, e1, 1, -8, 40)
    prolong(ub, vb, 1, -8, 40)
    sweep(vb, va, g0, e0, 0, -8, 72)
    sweep(va, last, g0, e0, 0, -8, 72)


def pack(m0, m1, to_west, to_east, index):
    lane = lanes_of(16)
    outer = lane % 64 < 32
    first = lane < 64
    turned = (lane >= 32) & (lane < 96)
    upper = m0[:16], turn(m1[:16], 64)
    lower = turn(m0[16:], 32), turn(m1[16:], 96)
    for k, target in enumerate((to_west, to_east)):
        a = jnp.where(first, upper[k], upper[1 - k])
        b = jnp.where(turned, lower[k], lower[1 - k])
        target[index] = jnp.where(outer, a, b) if k == 0 else jnp.where(outer, b, a)


def unpack(from_west, from_east, block, index, row):
    outer = lanes_of(16) % 64 < 32
    west, east = from_west[index], from_east[index]
    upper, lower = jnp.where(outer, east, west), jnp.where(outer, west, east)
    block[2, pl.ds(row, 16), :] = upper
    block[3, pl.ds(row, 16), :] = turn(upper, 64)
    block[2, pl.ds(row + 16, 16), :] = turn(lower, -32)
    block[3, pl.ds(row + 16, 16), :] = turn(lower, 32)


def kernel(
    perm_log, facies, scale_in, accumulation, previous, observed, cells_in, rates_in,
    pressure_out, adjoint_out, gradient_out,
    facies_scale, well_cells, well_rates, log_v, facies_v, observed_v, ext, ext2, to_west, to_east, from_west, from_east,
    to_west2, to_east2, from_west2, from_east2,
    f0, f1, f2, e0, e1, e2, g0, g1, g2, va, vb, r0, ua, ub, r1, wa, wb, pv, q, terms,
    load_sem, send0, recv0, send1, recv1, send2, recv2, send3, recv3,
):
    nx, ny, ns = lax.axis_size("gx"), lax.axis_size("gy"), lax.axis_size("scen")
    gx, gy, me = lax.axis_index("gx"), lax.axis_index("gy"), lax.axis_index("scen")
    north, south = lax.rem(gx + nx - 1, nx), lax.rem(gx + 1, nx)
    west, east = lax.rem(gy + ny - 1, ny), lax.rem(gy + 1, ny)
    around = [
        {"gx": north}, {"gx": south}, {"gy": west}, {"gy": east},
        {"gx": north, "gy": west}, {"gx": north, "gy": east},
        {"gx": south, "gy": west}, {"gx": south, "gy": east},
    ]
    peers = [{"scen": lax.rem(me + k, ns)} for k in sorted(range(1, ns), key=lambda k: -min(k, ns - k))]

    own = pl.ds(TOP[0], ROWS)
    loads = [
        pltpu.make_async_copy(perm_log, log_v, load_sem.at[0]),
        pltpu.make_async_copy(facies, facies_v, load_sem.at[1]),
        pltpu.make_async_copy(accumulation, ext.at[1, 0:2, own, :], load_sem.at[2]),
        pltpu.make_async_copy(previous.at[0], ext.at[2, 0:2, own, :], load_sem.at[3]),
        pltpu.make_async_copy(scale_in, facies_scale, load_sem.at[4]),
        pltpu.make_async_copy(cells_in, well_cells, load_sem.at[5]),
        pltpu.make_async_copy(rates_in, well_rates, load_sem.at[6]),
        pltpu.make_async_copy(observed.at[0], observed_v, load_sem.at[7]),
    ]
    always, westward, eastward = (0, 1), (4, 6, 2), (5, 7, 3)
    barrier = pltpu.get_barrier_semaphore()

    def greet(targets):
        for target in targets:
            pl.semaphore_signal(barrier, inc=1, device_id=target, device_id_type=MESH)

    def sideways(to_west, to_east):
        pl.when(gy > 0)(to_west)
        pl.when(gy < ny - 1)(to_east)

    sideways(lambda: greet([around[k] for k in westward]), lambda: greet([around[k] for k in eastward]))
    greet([around[k] for k in always] + peers)
    for copy in loads:
        copy.start()

    @pl.when(gy == 0)
    def _():
        from_west[...] = jnp.ones_like(from_west)
        from_west2[...] = jnp.ones_like(from_west2)

    @pl.when(gy == ny - 1)
    def _():
        from_east[...] = jnp.ones_like(from_east)
        from_east2[...] = jnp.ones_like(from_east2)

    for copy in loads[:7]:
        copy.wait()
    for layer in range(2):
        labels = facies_v[layer]
        factor = jnp.zeros((ROWS, LANES), jnp.float32)
        for label in range(FACIES):
            factor = jnp.where(labels == label, facies_scale[label], factor)
        ext[0, layer, own, :] = jnp.exp(log_v[layer]) * factor
    for field in range(3):
        for half in range(2):
            rows = pl.ds(TOP[0] + 32 * half, 32)
            pack(ext[field, 0, rows, :], ext[field, 1, rows, :], to_west, to_east, (field, pl.ds(16 * half, 16), slice(None)))
    no_west, no_east = lax.div(ny - gy, ny), lax.div(gy + 1, ny)
    pl.semaphore_wait(barrier, len(around) + len(peers) - 3 * (no_west + no_east))

    def exchange(block, w_out, e_out, w_in, e_in, send, recv):
        upper, lower = pl.ds(TOP[0], HALO), pl.ds(TOP[0] + ROWS - HALO, HALO)
        above, below = pl.ds(GUARD, HALO), pl.ds(TOP[0] + ROWS, HALO)
        first, second = pl.ds(0, 16), pl.ds(16, 16)
        lead = (slice(None),) * (len(w_out.shape) - 2)
        pairs = [
            (block.at[(*lead, slice(0, 2), upper)], block.at[(*lead, slice(0, 2), below)]),
            (block.at[(*lead, slice(0, 2), lower)], block.at[(*lead, slice(0, 2), above)]),
            (w_out, e_in.at[(*lead, pl.ds(16, 32))]),
            (e_out, w_in.at[(*lead, pl.ds(16, 32))]),
            (w_out.at[(*lead, first)], e_in.at[(*lead, pl.ds(48, 16))]),
            (e_out.at[(*lead, first)], w_in.at[(*lead, pl.ds(48, 16))]),
            (w_out.at[(*lead, second)], e_in.at[(*lead, pl.ds(0, 16))]),
            (e_out.at[(*lead, second)], w_in.at[(*lead, pl.ds(0, 16))]),
        ]
        copies = [
            pltpu.make_async_remote_copy(
                src_ref=source, dst_ref=target, send_sem=send.at[k], recv_sem=recv.at[k],
                device_id=around[k], device_id_type=MESH,
            )
            for k, (source, target) in enumerate(pairs)
        ]
        sideways(
            lambda: [copies[k].start() for k in westward] and None,
            lambda: [copies[k].start() for k in eastward] and None,
        )
        for k in always:
            copies[k].start()
        return copies

    def wait_recv(copies):
        for k in always:
            copies[k].wait_recv()
        sideways(
            lambda: [copies[k].wait_recv() for k in eastward] and None,
            lambda: [copies[k].wait_recv() for k in westward] and None,
        )

    first, rest = pl.ds(0, 1), pl.ds(1, 2)
    copies0, copies1 = [
        exchange(*[ref.at[part] for ref in (ext, to_west, to_east, from_west, from_east)], send, recv)
        for part, send, recv in ((first, send0, recv0), (rest, send1, recv1))
    ]
    plane, width = nx * ROWS * ny * LANES, ny * LANES

    def sources(row, count):
        lane = lanes_of(count)
        at = lax.broadcasted_iota(jnp.int32, (count, LANES), 0) + (row - TOP[0] + gx * ROWS)
        flat = at * width + lane + gy * LANES
        side = flat + jnp.where(lane >= 64, -LANES, LANES)
        for t, place in enumerate((flat, flat + plane, side, side + plane)):
            source = jnp.zeros((count, LANES), jnp.float32)
            for number in range(WELLS):
                source = source + jnp.where(place == well_cells[0, number], well_rates[0, number], 0.0)
            g0[t, pl.ds(row, count), :] = source

    over(0, -32, 96, sources)

    def receive(copies, fields):
        wait_recv(copies)
        for field in fields:
            for block in range(4):
                unpack(from_west, from_east, ext.at[field], (field, pl.ds(16 * block, 16), slice(None)), GUARD + 32 * block)

    receive(copies0, (0,))
    perm, accu, start = ext.at[0], ext.at[1], ext.at[2]
    fine_faces(perm, f0, gx, gy, nx, ny, -32, 96)
    coarsen(f0, f1, 1, -16, 48, (0, 1, 2))
    coarsen(f1, f2, 2, -8, 24, (0, 1, 2))
    receive(copies1, (1, 2))

    def right_side(row, count):
        rows = pl.ds(row, count)
        for t in range(TILES):
            value = accu[t, rows, :]
            f0[3, t, rows, :] = value
            g0[t, rows, :] = g0[t, rows, :] + value * start[t, rows, :]

    over(0, -32, 96, right_side)
    scale(f0, e0, 0, -32, 96)

    def weigh(row, count):
        rows = pl.ds(row, count)
        for t in range(TILES):
            g0[t, rows, :] = g0[t, rows, :] * e0[5, t, rows, :]

    over(0, -32, 96, weigh)
    coarsen(f0, f1, 1, -16, 48, (3,))
    coarsen(f1, f2, 2, -8, 24, (3,))
    scale(f1, e1, 1, -16, 48)
    scale(f2, e2, 2, -8, 24)
    levels = ((e0, g0), (e1, g1), (e2, g2))
    spare = (va, vb, r0, ua, ub, r1, wa, wb)
    sweep(start, va, g0, e0, 0, -32, 96)
    vcycle(levels, spare, pv)

    loads[7].wait()
    for layer in range(2):
        ext2[layer, own, :] = pv[layer, own, :] - observed_v[layer]
    for half in range(2):
        rows = pl.ds(TOP[0] + 32 * half, 32)
        pack(ext2[0, rows, :], ext2[1, rows, :], to_west2, to_east2, (pl.ds(16 * half, 16), slice(None)))
    copies2 = exchange(ext2, to_west2, to_east2, from_west2, from_east2, send2, recv2)
    pressure_out[0] = pv[0:2, own, :]

    def gradient_weights(row, count):
        lane = lanes_of(count)
        rows, before, after = pl.ds(row, count), pl.ds(row - 1, count), pl.ds(row + 1, count)
        p = tiles(pv, row, count)
        right, left = to_right(p, lane, 1), to_left(p, lane, 1)
        east = tiles(f0.at[0], row, count)
        west = to_left(east, lane, 1)
        for t in range(2):
            factor = -0.5 / perm[t, rows, :]
            south, north, across = f0[1, t, rows, :], f0[1, t, before, :], f0[2, t, rows, :]
            sides = (
                (north, pv[t, before, :], 1.0), (south, pv[t, after, :], 1.0), (east[t], right[t], 1.0),
                (west[t], left[t], 1.0), (across, p[t ^ 1], 1.0 / VERTICAL),
            )
            for k, (face, value, weight) in enumerate(sides):
                q[k, t, pl.ds(row - TOP[0], count), :] = factor * weight * (face * face) * (p[t] - value)

    over(0, 0, ROWS, gradient_weights)
    wait_recv(copies2)
    for block in range(4):
        unpack(from_west2, from_east2, ext2, (pl.ds(16 * block, 16), slice(None)), GUARD + 32 * block)

    def adjoint_side(row, count):
        for t in range(TILES):
            rows = pl.ds(row, count)
            value = e0[5, t, rows, :] * ext2[t, rows, :]
            g0[t, rows, :] = value
            va[t, rows, :] = value

    over(0, -32, 96, adjoint_side)
    vcycle(levels, spare, vb)
    adjoint_out[0] = vb[0:2, own, :]

    def gradient(row, count):
        lane = lanes_of(count)
        before, after = pl.ds(row - 1, count), pl.ds(row + 1, count)
        a = tiles(vb, row, count)
        right, left = to_right(a, lane, 1), to_left(a, lane, 1)
        rows = pl.ds(row - TOP[0], count)
        for t in range(2):
            near = q[0, t, rows, :] * (a[t] - vb[t, before, :]) + q[1, t, rows, :] * (a[t] - vb[t, after, :])
            side = q[2, t, rows, :] * (a[t] - right[t]) + q[3, t, rows, :] * (a[t] - left[t])
            terms[me, t, rows, :] = (near + side) + q[4, t, rows, :] * (a[t] - a[t ^ 1])

    over(0, 0, ROWS, gradient)
    part = terms.at[me]
    copies3 = [
        pltpu.make_async_remote_copy(
            src_ref=part, dst_ref=part, send_sem=send3.at[k], recv_sem=recv3.at[k],
            device_id=target, device_id_type=MESH,
        )
        for k, target in enumerate(peers)
    ]
    for copy in copies3:
        copy.start()
    for copy in copies3:
        copy.wait_recv()
    value = terms[0]
    for k in range(1, terms.shape[0]):
        value = value + terms[k]
    gradient_out[...] = value
    for copy in copies3:
        copy.wait_send()
    sent = (copies0, copies1, copies2)
    for copies in sent:
        for k in always:
            copies[k].wait_send()
    sideways(
        lambda: [copies[k].wait_send() for copies in sent for k in westward] and None,
        lambda: [copies[k].wait_send() for copies in sent for k in eastward] and None,
    )


def store(*refs):
    sem = refs[-1]
    copies = [pltpu.make_async_copy(refs[k], refs[k + 3], sem.at[k]) for k in range(3)]
    for copy in copies:
        copy.start()
    for copy in copies:
        copy.wait()


def shards(perm_log, facies, facies_scale, accumulation, previous, observed, well_cells, well_rates):
    ns = lax.axis_size("scen")
    f32 = jnp.float32
    block = (2, ROWS, LANES)
    anywhere = pl.BlockSpec(memory_space=pl.ANY)

    def vmem(*shape):
        return pltpu.VMEM(shape, f32)

    level = [(TILES, HEIGHT[k], LANES) for k in range(3)]
    dma = pltpu.SemaphoreType.DMA
    scratch = [
        pltpu.SMEM((FACIES,), f32), pltpu.SMEM((1, WELLS), jnp.int32), pltpu.SMEM((1, WELLS), f32),
        vmem(*block), pltpu.VMEM(block, jnp.int32), vmem(*block), vmem(3, *level[0]), vmem(*level[0]),
        vmem(3, 32, LANES), vmem(3, 32, LANES), vmem(3, 64, LANES), vmem(3, 64, LANES),
        vmem(32, LANES), vmem(32, LANES), vmem(64, LANES), vmem(64, LANES),
        *[vmem(4, *level[k]) for k in range(3)],
        *[vmem(7, *level[k]) for k in range(3)],
        *[vmem(*level[k]) for k in range(3)],
        *[vmem(*level[0]) for _ in range(3)],
        *[vmem(*level[1]) for _ in range(3)],
        *[vmem(*level[2]) for _ in range(2)],
        vmem(*level[0]), vmem(5, *block), vmem(ns, *block),
        *[dma((8,)) for _ in range(7)], dma((ns - 1,)), dma((ns - 1,)),
    ]
    shapes = ((1, *block), (1, *block), block)
    results = pl.pallas_call(
        kernel,
        out_shape=tuple(vmem(*shape) for shape in shapes),
        in_specs=[anywhere] * 8,
        out_specs=(pl.BlockSpec(memory_space=pltpu.VMEM),) * 3,
        scratch_shapes=scratch,
        compiler_params=pltpu.CompilerParams(
            collective_id=0, has_side_effects=True, vmem_limit_bytes=VMEM
        ),
    )(perm_log, facies, facies_scale, accumulation, previous, observed, well_cells, well_rates)
    return pl.pallas_call(
        store,
        out_shape=tuple(jax.ShapeDtypeStruct(shape, f32) for shape in shapes),
        in_specs=[anywhere] * 3,
        out_specs=(anywhere,) * 3,
        scratch_shapes=[dma((3,))],
        compiler_params=pltpu.CompilerParams(vmem_limit_bytes=2**20),
    )(*results)


def solution(mesh):
    return jax.shard_map(
        shards,
        mesh=mesh,
        in_specs=(
            P(None, "gx", "gy"),
            P(None, "gx", "gy"),
            P(),
            P(None, "gx", "gy"),
            P("scen", None, "gx", "gy"),
            P("scen", None, "gx", "gy"),
            P("scen", None),
            P("scen", None),
        ),
        out_specs=(P("scen", None, "gx", "gy"), P("scen", None, "gx", "gy"), P(None, "gx", "gy")),
        check_vma=False,
    )
```

```python
import jax
import jax.numpy as jnp
from jax import lax
from jax.experimental import pallas as pl
from jax.experimental.pallas import tpu as pltpu
from jax.sharding import PartitionSpec as P

WELLS = 5
FACIES = 4
VERTICAL = 0.3
DAMPING = 0.8
ROWS = 64
LANES = 128
HALO = 32
GUARD = 8
VMEM = 62 * 2**20
MESH = pl.DeviceIdType.MESH

TOP = (GUARD + HALO, GUARD + HALO // 2, GUARD + HALO // 4)
HEIGHT = tuple(ROWS // 2**k + 2 * TOP[k] for k in range(3))
CHUNK = 8
TILES = 4


def over(level, low, high, body, step=CHUNK):
    base = TOP[level]
    for row in range(low, high, step):
        body(base + row, min(step, high - row))


def lanes_of(count):
    return lax.broadcasted_iota(jnp.int32, (count, LANES), 1)


def turn(value, shift):
    return pltpu.roll(value, shift % LANES, 1)


def to_right(values, lane, s):
    wrapped = lane < s
    return [turn(jnp.where(wrapped, values[t ^ 2], values[t]), -s) for t in range(TILES)]


def to_left(values, lane, s):
    wrapped = lane >= LANES - s
    return [turn(jnp.where(wrapped, values[t ^ 2], values[t]), s) for t in range(TILES)]


def tiles(ref, row, count):
    return [ref[t, pl.ds(row, count), :] for t in range(TILES)]


def change(v, g, e, level, row, count):
    s = 2**level
    lane = lanes_of(count)
    mid = tiles(v, row, count)
    right, left = to_right(mid, lane, s), to_left(mid, lane, s)
    up = tiles(v, row - 1, count)
    down = tiles(v, row + 1, count)
    rows = pl.ds(row, count)
    out = []
    for t in range(TILES):
        near = e[0, t, rows, :] * up[t] + e[1, t, rows, :] * down[t]
        side = e[2, t, rows, :] * right[t] + e[3, t, rows, :] * left[t]
        out.append(
            (near + side) + (e[4, t, rows, :] * mid[t ^ 1] + (g[t, rows, :] - DAMPING * mid[t]))
        )
    return out, mid


def sweep(v, out, g, e, level, low, high):
    def body(row, count):
        delta, mid = change(v, g, e, level, row, count)
        for t in range(TILES):
            out[t, pl.ds(row, count), :] = mid[t] + delta[t]

    over(level, low, high, body)


def residual(v, out, g, e, level, low, high):
    def body(row, count):
        delta, _ = change(v, g, e, level, row, count)
        for t in range(TILES):
            out[t, pl.ds(row, count), :] = delta[t] * e[6, t, pl.ds(row, count), :]

    over(level, low, high, body)


def pair_sum(value, lane, s):
    return value + jnp.where(lane % (2 * s) < s, turn(value, -s), turn(value, s))


def even_odd(ref, index, row, count):
    first = ref[(*index, pl.ds(row, count, stride=2), slice(None))]
    second = ref[(*index, pl.ds(row + 1, count, stride=2), slice(None))]
    return first, second


def restrict(fine, g, e, level, low, high):
    s = 2 ** (level - 1)

    def body(row, count):
        lane = lanes_of(count)
        source = TOP[level - 1] + 2 * (row - TOP[level])
        for t in range(TILES):
            first, second = even_odd(fine, (t,), source, count)
            g[t, pl.ds(row, count), :] = pair_sum(first + second, lane, s) * e[5, t, pl.ds(row, count), :]

    over(level, low, high, body)


def prolong(coarse, fine, level, low, high):
    def body(row, count):
        target = TOP[level - 1] + 2 * (row - TOP[level])
        for t in range(TILES):
            value = coarse[t, pl.ds(row, count), :]
            for k in range(2):
                rows = pl.ds(target + k, count, stride=2)
                fine[t, rows, :] = fine[t, rows, :] + value

    over(level, low, high, body)


def coarsen(fine, coarse, level, low, high, members):
    s = 2 ** (level - 1)

    def body(row, count):
        lane = lanes_of(count)
        source = TOP[level - 1] + 2 * (row - TOP[level])
        rows = pl.ds(row, count)
        for k in members:
            for t in range(TILES):
                first, second = even_odd(fine, (k, t), source, count)
                if k == 0:
                    total = first + second
                    coarse[k, t, rows, :] = jnp.where(lane % (2 * s) < s, turn(total, -s), total)
                else:
                    coarse[k, t, rows, :] = pair_sum(second if k == 1 else first + second, lane, s)

    over(level, low, high, body)


def gather(faces, e, level, low, high):
    s = 2**level

    def body(row, count):
        lane = lanes_of(count)
        rows = pl.ds(row, count)
        east = tiles(faces.at[0], row, count)
        west = to_left(east, lane, s)
        for t in range(TILES):
            ends = faces[1, t, pl.ds(row - 1, count), :] + faces[1, t, rows, :]
            e[3, t, rows, :] = west[t]
            e[6, t, rows, :] = (ends + (east[t] + west[t])) + faces[2, t, rows, :]

    over(level, low, high, body)


def scale(faces, e, level, low, high):
    def body(row, count):
        rows = pl.ds(row, count)
        for t in range(TILES):
            diag = e[6, t, rows, :] + faces[3, t, rows, :]
            w = DAMPING / diag
            e[0, t, rows, :] = w * faces[1, t, pl.ds(row - 1, count), :]
            e[1, t, rows, :] = w * faces[1, t, rows, :]
            e[2, t, rows, :] = w * faces[0, t, rows, :]
            e[3, t, rows, :] = w * e[3, t, rows, :]
            e[4, t, rows, :] = w * faces[2, t, rows, :]
            e[5, t, rows, :] = w
            e[6, t, rows, :] = diag * (1.0 / DAMPING)

    over(level, low, high, body)


def harmonic(left, right):
    return 2.0 * left * right / (left + right)


def fine_faces(perm, faces, gx, gy, nx, ny, low, high):
    def body(row, count):
        lane = lanes_of(count)
        at = lax.broadcasted_iota(jnp.int32, (count, LANES), 0) + (row - TOP[0])
        own = tiles(perm, row, count)
        right = to_right(own, lane, 1)
        below = tiles(perm, row + 1, count)
        wall = ((at == -1) & (gx == 0)) | ((at == ROWS - 1) & (gx == nx - 1))
        last = lane == LANES - 1
        edges = (last & (gy == ny - 1), last & (gy == 0))
        rows = pl.ds(row, count)
        for t in range(TILES):
            faces[0, t, rows, :] = jnp.where(edges[t // 2], 0.0, harmonic(own[t], right[t]))
            faces[1, t, rows, :] = jnp.where(wall, 0.0, harmonic(own[t], below[t]))
        for t in (0, 2):
            between = VERTICAL * harmonic(own[t], own[t + 1])
            faces[2, t, rows, :] = between
            faces[2, t + 1, rows, :] = between

    over(0, low, high, body)


def vcycle(levels, spare, last):
    (e0, g0), (e1, g1), (e2, g2) = levels
    va, vb, r0, ua, ub, r1, wa, wb = spare
    sweep(va, vb, g0, e0, 0, -32, 96)
    residual(vb, r0, g0, e0, 0, -24, 88)
    restrict(r0, g1, e1, 1, -16, 48)
    sweep(g1, ub, g1, e1, 1, -16, 48)
    residual(ub, r1, g1, e1, 1, -16, 48)
    restrict(r1, g2, e2, 2, -8, 24)
    sweep(g2, wa, g2, e2, 2, -8, 24)
    sweep(wa, wb, g2, e2, 2, -8, 24)
    sweep(wb, wa, g2, e2, 2, -8, 24)
    prolong(wa, ub, 2, -4, 20)
    sweep(ub, ua, g1, e1, 1, -8, 40)
    sweep(ua, ub, g1, e1, 1, -8, 40)
    prolong(ub, vb, 1, -8, 40)
    sweep(vb, va, g0, e0, 0, -8, 72)
    sweep(va, last, g0, e0, 0, -8, 72)


def pack(m0, m1, to_west, to_east, index):
    lane = lanes_of(16)
    outer = lane % 64 < 32
    first = lane < 64
    turned = (lane >= 32) & (lane < 96)
    upper = m0[:16], turn(m1[:16], 64)
    lower = turn(m0[16:], 32), turn(m1[16:], 96)
    for k, target in enumerate((to_west, to_east)):
        a = jnp.where(first, upper[k], upper[1 - k])
        b = jnp.where(turned, lower[k], lower[1 - k])
        target[index] = jnp.where(outer, a, b) if k == 0 else jnp.where(outer, b, a)


def unpack(from_west, from_east, block, index, row):
    outer = lanes_of(16) % 64 < 32
    west, east = from_west[index], from_east[index]
    upper, lower = jnp.where(outer, east, west), jnp.where(outer, west, east)
    block[2, pl.ds(row, 16), :] = upper
    block[3, pl.ds(row, 16), :] = turn(upper, 64)
    block[2, pl.ds(row + 16, 16), :] = turn(lower, -32)
    block[3, pl.ds(row + 16, 16), :] = turn(lower, 32)


def kernel(
    perm_log, facies, scale_in, accumulation, previous, observed, cells_in, rates_in,
    pressure_out, adjoint_out, gradient_out,
    facies_scale, well_cells, well_rates, log_v, facies_v, observed_v, ext, ext2, to_west, to_east, from_west, from_east,
    to_west2, to_east2, from_west2, from_east2,
    f0, f1, f2, e0, e1, e2, g0, g1, g2, va, vb, r0, ua, ub, r1, wa, wb, pv, q, terms,
    load_sem, send0, recv0, send1, recv1, send2, recv2, send3, recv3,
):
    nx, ny, ns = lax.axis_size("gx"), lax.axis_size("gy"), lax.axis_size("scen")
    gx, gy, me = lax.axis_index("gx"), lax.axis_index("gy"), lax.axis_index("scen")
    north, south = lax.rem(gx + nx - 1, nx), lax.rem(gx + 1, nx)
    west, east = lax.rem(gy + ny - 1, ny), lax.rem(gy + 1, ny)
    around = [
        {"gx": north}, {"gx": south}, {"gy": west}, {"gy": east},
        {"gx": north, "gy": west}, {"gx": north, "gy": east},
        {"gx": south, "gy": west}, {"gx": south, "gy": east},
    ]
    peers = [{"scen": lax.rem(me + k, ns)} for k in sorted(range(1, ns), key=lambda k: -min(k, ns - k))]

    own = pl.ds(TOP[0], ROWS)
    loads = [
        pltpu.make_async_copy(perm_log, log_v, load_sem.at[0]),
        pltpu.make_async_copy(facies, facies_v, load_sem.at[1]),
        pltpu.make_async_copy(accumulation, ext.at[1, 0:2, own, :], load_sem.at[2]),
        pltpu.make_async_copy(previous.at[0], ext.at[2, 0:2, own, :], load_sem.at[3]),
        pltpu.make_async_copy(scale_in, facies_scale, load_sem.at[4]),
        pltpu.make_async_copy(cells_in, well_cells, load_sem.at[5]),
        pltpu.make_async_copy(rates_in, well_rates, load_sem.at[6]),
        pltpu.make_async_copy(observed.at[0], observed_v, load_sem.at[7]),
    ]
    always, westward, eastward = (0, 1), (4, 6, 2), (5, 7, 3)
    barrier = pltpu.get_barrier_semaphore()

    def greet(targets):
        for target in targets:
            pl.semaphore_signal(barrier, inc=1, device_id=target, device_id_type=MESH)

    def sideways(to_west, to_east):
        pl.when(gy > 0)(to_west)
        pl.when(gy < ny - 1)(to_east)

    sideways(lambda: greet([around[k] for k in westward]), lambda: greet([around[k] for k in eastward]))
    greet([around[k] for k in always] + peers)
    for copy in loads:
        copy.start()

    @pl.when(gy == 0)
    def _():
        from_west[...] = jnp.ones_like(from_west)
        from_west2[...] = jnp.ones_like(from_west2)

    @pl.when(gy == ny - 1)
    def _():
        from_east[...] = jnp.ones_like(from_east)
        from_east2[...] = jnp.ones_like(from_east2)

    for copy in loads[:7]:
        copy.wait()
    for layer in range(2):
        labels = facies_v[layer]
        factor = jnp.zeros((ROWS, LANES), jnp.float32)
        for label in range(FACIES):
            factor = jnp.where(labels == label, facies_scale[label], factor)
        ext[0, layer, own, :] = jnp.exp(log_v[layer]) * factor
    for field in range(3):
        for half in range(2):
            rows = pl.ds(TOP[0] + 32 * half, 32)
            pack(ext[field, 0, rows, :], ext[field, 1, rows, :], to_west, to_east, (field, pl.ds(16 * half, 16), slice(None)))
    no_west, no_east = lax.div(ny - gy, ny), lax.div(gy + 1, ny)
    pl.semaphore_wait(barrier, len(around) + len(peers) - 3 * (no_west + no_east))

    def exchange(block, w_out, e_out, w_in, e_in, send, recv):
        upper, lower = pl.ds(TOP[0], HALO), pl.ds(TOP[0] + ROWS - HALO, HALO)
        above, below = pl.ds(GUARD, HALO), pl.ds(TOP[0] + ROWS, HALO)
        first, second = pl.ds(0, 16), pl.ds(16, 16)
        lead = (slice(None),) * (len(w_out.shape) - 2)
        pairs = [
            (block.at[(*lead, slice(0, 2), upper)], block.at[(*lead, slice(0, 2), below)]),
            (block.at[(*lead, slice(0, 2), lower)], block.at[(*lead, slice(0, 2), above)]),
            (w_out, e_in.at[(*lead, pl.ds(16, 32))]),
            (e_out, w_in.at[(*lead, pl.ds(16, 32))]),
            (w_out.at[(*lead, first)], e_in.at[(*lead, pl.ds(48, 16))]),
            (e_out.at[(*lead, first)], w_in.at[(*lead, pl.ds(48, 16))]),
            (w_out.at[(*lead, second)], e_in.at[(*lead, pl.ds(0, 16))]),
            (e_out.at[(*lead, second)], w_in.at[(*lead, pl.ds(0, 16))]),
        ]
        copies = [
            pltpu.make_async_remote_copy(
                src_ref=source, dst_ref=target, send_sem=send.at[k], recv_sem=recv.at[k],
                device_id=around[k], device_id_type=MESH,
            )
            for k, (source, target) in enumerate(pairs)
        ]
        sideways(
            lambda: [copies[k].start() for k in westward] and None,
            lambda: [copies[k].start() for k in eastward] and None,
        )
        for k in always:
            copies[k].start()
        return copies

    def wait_recv(copies):
        for k in always:
            copies[k].wait_recv()
        sideways(
            lambda: [copies[k].wait_recv() for k in eastward] and None,
            lambda: [copies[k].wait_recv() for k in westward] and None,
        )

    first, rest = pl.ds(0, 1), pl.ds(1, 2)
    copies0, copies1 = [
        exchange(*[ref.at[part] for ref in (ext, to_west, to_east, from_west, from_east)], send, recv)
        for part, send, recv in ((first, send0, recv0), (rest, send1, recv1))
    ]
    plane, width = nx * ROWS * ny * LANES, ny * LANES

    def sources(row, count):
        lane = lanes_of(count)
        at = lax.broadcasted_iota(jnp.int32, (count, LANES), 0) + (row - TOP[0] + gx * ROWS)
        flat = at * width + lane + gy * LANES
        side = flat + jnp.where(lane >= 64, -LANES, LANES)
        for t, place in enumerate((flat, flat + plane, side, side + plane)):
            source = jnp.zeros((count, LANES), jnp.float32)
            for number in range(WELLS):
                source = source + jnp.where(place == well_cells[0, number], well_rates[0, number], 0.0)
            g0[t, pl.ds(row, count), :] = source

    over(0, -32, 96, sources)

    def receive(copies, fields):
        wait_recv(copies)
        for field in fields:
            for block in range(4):
                unpack(from_west, from_east, ext.at[field], (field, pl.ds(16 * block, 16), slice(None)), GUARD + 32 * block)

    receive(copies0, (0,))
    perm, accu, start = ext.at[0], ext.at[1], ext.at[2]
    fine_faces(perm, f0, gx, gy, nx, ny, -32, 96)
    coarsen(f0, f1, 1, -16, 48, (0, 1, 2))
    coarsen(f1, f2, 2, -8, 24, (0, 1, 2))
    gather(f0, e0, 0, -32, 96)
    gather(f1, e1, 1, -16, 48)
    gather(f2, e2, 2, -8, 24)
    receive(copies1, (1, 2))

    def right_side(row, count):
        rows = pl.ds(row, count)
        for t in range(TILES):
            value = accu[t, rows, :]
            f0[3, t, rows, :] = value
            g0[t, rows, :] = g0[t, rows, :] + value * start[t, rows, :]

    over(0, -32, 96, right_side)
    scale(f0, e0, 0, -32, 96)

    def weigh(row, count):
        rows = pl.ds(row, count)
        for t in range(TILES):
            g0[t, rows, :] = g0[t, rows, :] * e0[5, t, rows, :]

    over(0, -32, 96, weigh)
    coarsen(f0, f1, 1, -16, 48, (3,))
    coarsen(f1, f2, 2, -8, 24, (3,))
    scale(f1, e1, 1, -16, 48)
    scale(f2, e2, 2, -8, 24)
    levels = ((e0, g0), (e1, g1), (e2, g2))
    spare = (va, vb, r0, ua, ub, r1, wa, wb)
    sweep(start, va, g0, e0, 0, -32, 96)
    vcycle(levels, spare, pv)

    loads[7].wait()
    for layer in range(2):
        ext2[layer, own, :] = pv[layer, own, :] - observed_v[layer]
    for half in range(2):
        rows = pl.ds(TOP[0] + 32 * half, 32)
        pack(ext2[0, rows, :], ext2[1, rows, :], to_west2, to_east2, (pl.ds(16 * half, 16), slice(None)))
    copies2 = exchange(ext2, to_west2, to_east2, from_west2, from_east2, send2, recv2)
    pressure_out[0] = pv[0:2, own, :]

    def gradient_weights(row, count):
        lane = lanes_of(count)
        rows, before, after = pl.ds(row, count), pl.ds(row - 1, count), pl.ds(row + 1, count)
        p = tiles(pv, row, count)
        right, left = to_right(p, lane, 1), to_left(p, lane, 1)
        east = tiles(f0.at[0], row, count)
        west = to_left(east, lane, 1)
        for t in range(2):
            factor = -0.5 / perm[t, rows, :]
            south, north, across = f0[1, t, rows, :], f0[1, t, before, :], f0[2, t, rows, :]
            sides = (
                (north, pv[t, before, :], 1.0), (south, pv[t, after, :], 1.0), (east[t], right[t], 1.0),
                (west[t], left[t], 1.0), (across, p[t ^ 1], 1.0 / VERTICAL),
            )
            for k, (face, value, weight) in enumerate(sides):
                q[k, t, pl.ds(row - TOP[0], count), :] = factor * weight * (face * face) * (p[t] - value)

    over(0, 0, ROWS, gradient_weights)
    wait_recv(copies2)
    for block in range(4):
        unpack(from_west2, from_east2, ext2, (pl.ds(16 * block, 16), slice(None)), GUARD + 32 * block)

    def adjoint_side(row, count):
        for t in range(TILES):
            rows = pl.ds(row, count)
            value = e0[5, t, rows, :] * ext2[t, rows, :]
            g0[t, rows, :] = value
            va[t, rows, :] = value

    over(0, -32, 96, adjoint_side)
    vcycle(levels, spare, vb)
    adjoint_out[0] = vb[0:2, own, :]

    def gradient(row, count):
        lane = lanes_of(count)
        before, after = pl.ds(row - 1, count), pl.ds(row + 1, count)
        a = tiles(vb, row, count)
        right, left = to_right(a, lane, 1), to_left(a, lane, 1)
        rows = pl.ds(row - TOP[0], count)
        for t in range(2):
            near = q[0, t, rows, :] * (a[t] - vb[t, before, :]) + q[1, t, rows, :] * (a[t] - vb[t, after, :])
            side = q[2, t, rows, :] * (a[t] - right[t]) + q[3, t, rows, :] * (a[t] - left[t])
            terms[me, t, rows, :] = (near + side) + q[4, t, rows, :] * (a[t] - a[t ^ 1])

    over(0, 0, ROWS, gradient)
    part = terms.at[me]
    copies3 = [
        pltpu.make_async_remote_copy(
            src_ref=part, dst_ref=part, send_sem=send3.at[k], recv_sem=recv3.at[k],
            device_id=target, device_id_type=MESH,
        )
        for k, target in enumerate(peers)
    ]
    for copy in copies3:
        copy.start()
    for copy in copies3:
        copy.wait_recv()
    value = terms[0]
    for k in range(1, terms.shape[0]):
        value = value + terms[k]
    gradient_out[...] = value
    for copy in copies3:
        copy.wait_send()
    sent = (copies0, copies1, copies2)
    for copies in sent:
        for k in always:
            copies[k].wait_send()
    sideways(
        lambda: [copies[k].wait_send() for copies in sent for k in westward] and None,
        lambda: [copies[k].wait_send() for copies in sent for k in eastward] and None,
    )


def store(*refs):
    sem = refs[-1]
    copies = [pltpu.make_async_copy(refs[k], refs[k + 3], sem.at[k]) for k in range(3)]
    for copy in copies:
        copy.start()
    for copy in copies:
        copy.wait()


def shards(perm_log, facies, facies_scale, accumulation, previous, observed, well_cells, well_rates):
    ns = lax.axis_size("scen")
    f32 = jnp.float32
    block = (2, ROWS, LANES)
    anywhere = pl.BlockSpec(memory_space=pl.ANY)

    def vmem(*shape):
        return pltpu.VMEM(shape, f32)

    level = [(TILES, HEIGHT[k], LANES) for k in range(3)]
    dma = pltpu.SemaphoreType.DMA
    scratch = [
        pltpu.SMEM((FACIES,), f32), pltpu.SMEM((1, WELLS), jnp.int32), pltpu.SMEM((1, WELLS), f32),
        vmem(*block), pltpu.VMEM(block, jnp.int32), vmem(*block), vmem(3, *level[0]), vmem(*level[0]),
        vmem(3, 32, LANES), vmem(3, 32, LANES), vmem(3, 64, LANES), vmem(3, 64, LANES),
        vmem(32, LANES), vmem(32, LANES), vmem(64, LANES), vmem(64, LANES),
        *[vmem(4, *level[k]) for k in range(3)],
        *[vmem(7, *level[k]) for k in range(3)],
        *[vmem(*level[k]) for k in range(3)],
        *[vmem(*level[0]) for _ in range(3)],
        *[vmem(*level[1]) for _ in range(3)],
        *[vmem(*level[2]) for _ in range(2)],
        vmem(*level[0]), vmem(5, *block), vmem(ns, *block),
        *[dma((8,)) for _ in range(7)], dma((ns - 1,)), dma((ns - 1,)),
    ]
    shapes = ((1, *block), (1, *block), block)
    results = pl.pallas_call(
        kernel,
        out_shape=tuple(vmem(*shape) for shape in shapes),
        in_specs=[anywhere] * 8,
        out_specs=(pl.BlockSpec(memory_space=pltpu.VMEM),) * 3,
        scratch_shapes=scratch,
        compiler_params=pltpu.CompilerParams(
            collective_id=0, has_side_effects=True, vmem_limit_bytes=VMEM
        ),
    )(perm_log, facies, facies_scale, accumulation, previous, observed, well_cells, well_rates)
    return pl.pallas_call(
        store,
        out_shape=tuple(jax.ShapeDtypeStruct(shape, f32) for shape in shapes),
        in_specs=[anywhere] * 3,
        out_specs=(anywhere,) * 3,
        scratch_shapes=[dma((3,))],
        compiler_params=pltpu.CompilerParams(vmem_limit_bytes=2**20),
    )(*results)


def solution(mesh):
    return jax.shard_map(
        shards,
        mesh=mesh,
        in_specs=(
            P(None, "gx", "gy"),
            P(None, "gx", "gy"),
            P(),
            P(None, "gx", "gy"),
            P("scen", None, "gx", "gy"),
            P("scen", None, "gx", "gy"),
            P("scen", None),
            P("scen", None),
        ),
        out_specs=(P("scen", None, "gx", "gy"), P("scen", None, "gx", "gy"), P(None, "gx", "gy")),
        check_vma=False,
    )
```
